256 devices in a mesh: gx: 16 (over x, y), gy: 4 (over z_lo), gz: 4 (over z_hi, core).
Axes of the slice: x: 4, y: 4, z: 8 (z_hi: 2, z_lo: 4; z = z_hi * 4 + z_lo), core: 2. Of those that a mesh axis runs over, the one named last changes fastest.
Arguments:
- adjoint: float32 [19, 256, 32, 512], P(None, 'gx', 'gz', 'gy'), may hold values from -6 to 6
- density: float32 [256, 32, 512], P('gx', 'gz', 'gy'), may hold values from 0.8 to 1.2
- velocity: float32 [3, 256, 32, 512], P(None, 'gx', 'gz', 'gy'), may hold values from -0.4 to 0.4
- porosity: float32 [256, 32, 512], P('gx', 'gz', 'gy'), may hold values from 0.05 to 1
- node_type: int32 [256, 32, 512], P('gx', 'gz', 'gy'), may hold values from 0 to 2
- sensitivity_in: float32 [256, 32, 512], P('gx', 'gz', 'gy'), may hold values from -6 to 6
Outputs:
- adjoint_out: float32 [19, 256, 32, 512], P(None, 'gx', 'gz', 'gy')
- sensitivity: float32 [256, 32, 512], P('gx', 'gz', 'gy')
The draws below stay inside these ranges and needn't reach their ends.
Inputs may be any that keep to these rules, and one draw needn't show every extreme that they name: `node_type`: 0 fluid, 1 inlet forcing, 2 fixed wall.
All inputs are finite; a program needn't handle non-finite values.
Results may differ from the reference program's by a relative error of at most 0.0001.
Values sent between devices are 32-bit elements; how exact they have to be, the bound alone decides.
A program may use at most 128 MiB of HBM per device.

```python
import jax
import jax.numpy as jnp
import numpy as np
from jax import lax

Q = 19
STEPS = 2
CX = 16
NX = 256
NY = 512
NZ = 32


def place_ends(values, rng, smallest, high):
    index_at = [jax.random.randint(jax.random.fold_in(rng, axis), (), 0, length) for axis, length in enumerate(values.shape)]
    longest = values.shape.index(max(values.shape))
    neighbour = index_at[:longest] + [(index_at[longest] + 1) % values.shape[longest]] + index_at[longest + 1:]
    return values.at[tuple(index_at)].set(smallest).at[tuple(neighbour)].set(high)


def steps_of(stream_key, extent, cuts, low, high):
    def one(position, blocks):
        heights = jax.random.uniform(jax.random.fold_in(jax.random.fold_in(stream_key, 6), position), (blocks,), jnp.float32, low / len(cuts), high / len(cuts))
        return jnp.repeat(jnp.exp(heights), extent[position] // blocks).reshape((-1,) + (1,) * (len(extent) - position - 1))

    level = one(*cuts[0])
    for cut in cuts[1:]:
        level = level * one(*cut)
    return level


def scatter_about(key, extent, width, bound, shards=(), kind=jnp.bfloat16):
    values = width * jax.random.normal(key, extent, jnp.float32)
    if shards:
        values = values * steps_of(key, extent, shards, -0.22, 0.18)
    return jnp.clip(values, -bound, bound).astype(kind)


def setup_inputs(seed: int = 0) -> dict:
    keys = jax.random.split(jax.random.key(seed), 7)
    adjoint = scatter_about(keys[0], (Q, NX, NZ, NY), 1.0, 6.0, ((1, 16), (2, 4), (3, 4)), jnp.float32)
    density = jnp.clip(0.8 + 0.40000004 * jax.random.uniform(keys[1], (NX, NZ, NY), jnp.float32) ** steps_of(keys[1], (NX, NZ, NY), ((0, 16), (1, 4), (2, 4)), -0.2, 0.2), 0.8, 1.2)
    velocity = scatter_about(keys[2], (3, NX, NZ, NY), 0.12, 0.4, ((1, 16), (2, 4), (3, 4)), jnp.float32)
    porosity = jnp.clip(0.05 + 0.95 * jax.random.uniform(keys[3], (NX, NZ, NY), jnp.float32) ** steps_of(keys[3], (NX, NZ, NY), ((0, 16), (1, 4), (2, 4)), -0.2, 0.2), 0.05, 1.0)
    node_type = place_ends(jax.random.randint(keys[4], (NX, NZ, NY), 0, 3), jax.random.fold_in(keys[4], 1), 0, 2).astype(jnp.int32)
    sensitivity_in = scatter_about(keys[5], (NX, NZ, NY), 1.0, 6.0, ((0, 16), (1, 4), (2, 4)), jnp.float32)
    return {"adjoint": adjoint, "density": density, "velocity": velocity, "porosity": porosity, "node_type": node_type, "sensitivity_in": sensitivity_in}


def lattice_tables():
    velocities = [(0, 0, 0), (1, 0, 0), (-1, 0, 0), (0, 1, 0), (0, -1, 0), (0, 0, 1), (0, 0, -1),
                  (1, 1, 0), (-1, -1, 0), (1, -1, 0), (-1, 1, 0), (1, 0, 1), (-1, 0, -1), (1, 0, -1), (-1, 0, 1),
                  (0, 1, 1), (0, -1, -1), (0, 1, -1), (0, -1, 1)]
    lattice = np.array(velocities) * 1.0
    weights = np.array([1.0 / 3.0] + [1.0 / 18.0] * 6 + [1.0 / 36.0] * 12)
    px, py, pz = lattice[:, 0], lattice[:, 1], lattice[:, 2]
    polys = [np.ones(19), px, py, pz, px * px, py * py, pz * pz, px * py, px * pz, py * pz,
             px * px * py, px * px * pz, py * py * px, py * py * pz, pz * pz * px, pz * pz * py,
             px * px * py * py, px * px * pz * pz, py * py * pz * pz]
    basis = []
    for poly in polys:
        vector = poly.copy()
        for prior in basis:
            vector = vector - np.sum(weights * vector * prior) / np.sum(weights * prior * prior) * prior
        basis.append(vector)
    moments = np.stack(basis)
    norms = np.sum(moments * moments * weights[None, :], axis=1)
    inverse = weights[:, None] * moments.T / norms[None, :]
    rates = np.array([1.0] * 4 + [1.6] * 6 + [1.2] * 6 + [1.4] * 3)
    relax = inverse @ (rates[:, None] * moments)
    opposite = [velocities.index((-a, -b, -c)) for (a, b, c) in velocities]
    return relax, lattice, weights, opposite, velocities


def adjoint_collide(pulled, density, velocity, porosity, inlet, wall, tables):
    relax_np, lattice_np, weights_np, opposite, velocities = tables
    highest = lax.Precision.HIGHEST
    relax = jnp.asarray(relax_np, dtype=jnp.float32)
    lattice = jnp.asarray(lattice_np, dtype=jnp.float32)
    weights = jnp.asarray(weights_np, dtype=jnp.float32).reshape(19, 1, 1, 1)
    hvals = jnp.einsum('iq,ixzy->qxzy', relax, pulled, precision=highest)
    cu = jnp.einsum('id,dxzy->ixzy', lattice, velocity, precision=highest)
    usq = jnp.sum(velocity * velocity, axis=0)
    weighted = weights * hvals
    hzero = jnp.sum(weighted, axis=0)
    huu = jnp.sum(weighted * cu * cu, axis=0)
    hcvec = jnp.einsum('id,ixzy->dxzy', lattice, weighted, precision=highest)
    hcuvec = jnp.einsum('id,ixzy->dxzy', lattice, weighted * cu, precision=highest)
    gsq = porosity * porosity
    vector = 3.0 * porosity * hcvec + 9.0 * gsq * hcuvec - 3.0 * gsq * hzero * velocity
    scalar = hzero * (1.0 + 1.5 * gsq * usq) - 4.5 * gsq * huu
    fluid = pulled - hvals + scalar + jnp.einsum('kd,dxzy->kxzy', lattice, vector, precision=highest)
    fluid = fluid + jnp.where(inlet, lattice[:, 0].reshape(19, 1, 1, 1), jnp.float32(0.0))
    bounced = pulled[np.array(opposite)]
    updated = jnp.where(wall, bounced, fluid)
    gain = density * jnp.sum(weighted * (3.0 * cu + 9.0 * porosity * cu * cu - 3.0 * porosity * usq), axis=0)
    gain = jnp.where(wall, jnp.float32(0.0), gain)
    return updated, gain


def reference(adjoint, density, velocity, porosity, node_type, sensitivity_in):
    tables = lattice_tables()
    velocities = tables[4]
    blocks = NX // CX

    def split(field):
        lead = field.shape[:-3]
        shaped = field.reshape(lead + (blocks, CX, NZ, NY))
        return jnp.moveaxis(shaped, len(lead), 0)

    def merge(field):
        moved = jnp.moveaxis(field, 0, field.ndim - 4)
        return moved.reshape(moved.shape[:-4] + (NX, NZ, NY))

    current = adjoint
    sensitivity = sensitivity_in
    inlet = split(node_type == 1)
    wall = split(node_type == 2)
    for step in range(STEPS):
        pulled = jnp.stack([jnp.roll(current[j], (-velocities[j][0], -velocities[j][2], -velocities[j][1]), axis=(0, 1, 2)) for j in range(19)])

        def one_block(items):
            return adjoint_collide(items[0], items[1], items[2], items[3], items[4], items[5], tables)

        updated, gain = lax.map(one_block, (split(pulled), split(density), split(velocity), split(porosity), inlet, wall))
        current = merge(updated)
        sensitivity = sensitivity + merge(gain)
    return current, sensitivity
```

```python
import functools

import jax
import jax.numpy as jnp
from jax import lax
from jax.experimental import pallas as pl
from jax.experimental.pallas import tpu as pltpu
from jax.sharding import PartitionSpec as P

AXES = ("gx", "gy", "gz")
PX, PZ, PY = 16, 8, 128
ROWS = PX * PZ

VELOCITIES = [
    (0, 0, 0),
    (1, 0, 0),
    (-1, 0, 0),
    (0, 1, 0),
    (0, -1, 0),
    (0, 0, 1),
    (0, 0, -1),
    (1, 1, 0),
    (-1, -1, 0),
    (1, -1, 0),
    (-1, 1, 0),
    (1, 0, 1),
    (-1, 0, -1),
    (1, 0, -1),
    (-1, 0, 1),
    (0, 1, 1),
    (0, -1, -1),
    (0, 1, -1),
    (0, -1, 1),
]
CROSS = [[[i for i, c in enumerate(VELOCITIES) if c[a] == s] for s in (1, -1)] for a in range(3)]
CROSS_X, CROSS_Y, CROSS_Z = CROSS
FACES_X = [(-1, 0, 0), (1, 0, 0)]
FACES_Y = [(0, -1, 0), (0, 1, 0)]
FACES_Z = [(0, 0, -1), (0, 0, 1)]
EDGES_XY = [(a, b, 0) for a in (-1, 1) for b in (-1, 1)]
EDGES_YZ = [(0, a, b) for a in (-1, 1) for b in (-1, 1)]
EDGES_XZ = [(a, 0, b) for a in (-1, 1) for b in (-1, 1)]
ROUTES = FACES_Z + EDGES_YZ + EDGES_XZ + FACES_Y + EDGES_XY + FACES_X


def side(sign):
    return (sign + 1) // 2


def collide(p, rho, u, g, node):
    ux, uy, uz = u
    e = [p[i] + p[i + 1] for i in range(1, 19, 2)]
    o = [p[i] - p[i + 1] for i in range(1, 19, 2)]
    sxy, sxz, syz = e[3] + e[4], e[5] + e[6], e[7] + e[8]
    dxy, dxz, dyz = e[3] - e[4], e[5] - e[6], e[7] - e[8]
    sx = 2.0 * e[0] + (sxy + sxz)
    sy = 2.0 * e[1] + (sxy + syz)
    sz = 2.0 * e[2] + (sxz + syz)
    trace = sx + sy + sz
    h36 = 12.0 * p[0] + (trace - (sxy + sxz + syz))
    third = h36 * (1.0 / 3.0)
    mxx, myy, mzz = sx - third, sy - third, sz - third
    hcx = 2.0 * o[0] + ((o[3] + o[4]) + (o[5] + o[6]))
    hcy = 2.0 * o[1] + ((o[3] - o[4]) + (o[7] + o[8]))
    hcz = 2.0 * o[2] + ((o[5] - o[6]) + (o[7] - o[8]))
    nx = mxx * ux + dxy * uy + dxz * uz
    ny = dxy * ux + myy * uy + dyz * uz
    nz = dxz * ux + dyz * uy + mzz * uz
    q = ux * nx + uy * ny + uz * nz
    first = ux * hcx + uy * hcy + uz * hcz
    g4 = 0.4 * g
    b = g4 * g
    a = g * (1.0 / 12.0) + (1.0 / 60.0)
    gain = rho * (first * (1.0 / 12.0) + g4 * q)
    inlet = node == 1
    wall = node == 2
    vx = a * hcx + b * nx + jnp.where(inlet, 1.0, 0.0)
    vy = a * hcy + b * ny
    vz = a * hcz + b * nz
    base = h36 * (1.1 / 36.0) + trace * (1.0 / 120.0) - (0.5 * b) * q
    ex, ey, ez = -0.025 * mxx, -0.025 * myy, -0.025 * mzz
    bx, by = base + ex, base + ey
    bz = base + ez
    bxy, bxz, byz = bx + ey, bx + ez, by + ez
    wxy, wxz, wyz = 0.05 * dxy, 0.05 * dxz, 0.05 * dyz
    even = [bx, by, bz, bxy - wxy, bxy + wxy, bxz - wxz, bxz + wxz, byz - wyz, byz + wyz]
    odd = [vx, vy, vz, vx + vy, vx - vy, vx + vz, vx - vz, vy + vz, vy - vz]
    new = [jnp.where(wall, p[0], base - 0.4 * p[0])]
    for k in range(9):
        up = even[k] - 0.2 * e[k]
        down = odd[k] - 0.1 * o[k]
        new.append(jnp.where(wall, p[2 * k + 2], up + down))
        new.append(jnp.where(wall, p[2 * k + 1], up - down))
    return new, jnp.where(wall, 0.0, gain)


def lattice_kernel(
    adj_hbm,
    rho_hbm,
    vel_hbm,
    por_hbm,
    node_hbm,
    sens_hbm,
    out_hbm,
    out_sens_hbm,
    field,
    rho,
    vel,
    por,
    node,
    sens,
    result,
    x_out,
    y_out,
    z_out,
    x_in,
    y_in,
    z_in,
    xy_in,
    yz_in,
    xz_in,
    load_sem,
    store_sem,
    send_sem,
    recv_sem,
):
    here = [lax.axis_index(a) for a in AXES]
    size = [lax.axis_size(a) for a in AXES]

    def device(route):
        return tuple(lax.rem(h + (d + n), n) if d else h for h, d, n in zip(here, route, size))

    barrier = pltpu.get_barrier_semaphore()
    for route in ROUTES:
        pl.semaphore_signal(
            barrier, inc=1, device_id=device(route), device_id_type=pl.DeviceIdType.MESH
        )
    own = pl.ds(PZ, ROWS)
    loads = [
        pltpu.make_async_copy(src, dst, load_sem.at[k])
        for k, (src, dst) in enumerate(
            [
                (adj_hbm, field.at[0, :, own, :]),
                (rho_hbm, rho),
                (vel_hbm, vel),
                (por_hbm, por),
                (node_hbm, node),
                (sens_hbm, sens),
            ]
        )
    ]
    for copy in loads:
        copy.start()

    lane = lax.broadcasted_iota(jnp.int32, (PZ, PY), 1)
    row = lax.broadcasted_iota(jnp.int32, (PZ, PY), 0)

    def plane(x):
        return pl.ds(pl.multiple_of(x * PZ, PZ), PZ)

    def columns(values, x, tiles):
        made = []
        for s in range(2):
            tile = tiles[s]
            for j, i in enumerate(CROSS_Y[s]):
                at = x + j * PX
                turned = pltpu.roll(values(i), at if s == 0 else at + 1, axis=1)
                tile = jnp.where(lane == at, turned, tile)
            made.append(tile)
        return tuple(made)

    def exchange(step, tiles):
        for s in range(2):
            y_out[step, s] = tiles[s]
            for j, i in enumerate(CROSS_Z[s]):
                z_out[step, s, j] = field[step, i, pl.ds(PZ + s * (PZ - 1), PX, stride=PZ), :]
            for j, i in enumerate(CROSS_X[s]):
                x_out[step, s, j] = field[step, i, pl.ds(PZ * (PX if s else 1), PZ), :]
        if step == 0:
            pl.semaphore_wait(barrier, len(ROUTES))
        copies = {}
        for k, route in enumerate(ROUTES):
            dx, dy, dz = route
            if route in FACES_X:
                src, dst = x_out.at[step, side(dx)], x_in.at[step, side(dx)]
            elif route in FACES_Z:
                src, dst = z_out.at[step, side(dz)], z_in.at[step, side(dz)]
            elif route in FACES_Y:
                src, dst = y_out.at[step, side(dy)], y_in.at[step, side(dy)]
            elif route in EDGES_XY:
                src, dst = y_out.at[step, side(dy)], xy_in.at[step, side(dx), side(dy)]
            elif route in EDGES_YZ:
                src, dst = y_out.at[step, side(dy)], yz_in.at[step, side(dy), side(dz)]
            else:
                j = CROSS_Z[side(dz)].index(VELOCITIES.index((-dx, 0, -dz)))
                src = z_out.at[step, side(dz), j, pl.ds(side(dx) * (PX - 8), 8), :]
                dst = xz_in.at[step, side(dx), side(dz)]
            copy = pltpu.make_async_remote_copy(
                src_ref=src,
                dst_ref=dst,
                send_sem=send_sem.at[step, k],
                recv_sem=recv_sem.at[step, k],
                device_id=device(route),
                device_id_type=pl.DeviceIdType.MESH,
            )
            copy.start()
            copies[route] = copy
        return copies

    def insert(step, copies):
        for route in ROUTES:
            copies[route].wait_recv()
        for s in range(2):
            for j, i in enumerate(CROSS_X[s]):
                field[step, i, pl.ds(0 if s else PZ * (PX + 1), PZ), :] = x_in[step, s, j]
            for j, i in enumerate(CROSS_Z[s]):
                field[step, i, pl.ds(PZ + s * (PZ - 1), PX, stride=PZ), :] = z_in[step, s, j]
        for dx, _, dz in EDGES_XZ:
            i = VELOCITIES.index((-dx, 0, -dz))
            at = (0 if dx == 1 else PZ * (PX + 1)) + side(dz) * (PZ - 1)
            field[step, i, pl.ds(at, 1), :] = xz_in[
                step, side(dx), side(dz), pl.ds(side(dx) * (PZ - 1), 1), :
            ]
        halos = []
        for s in range(2):
            tile = y_in[step, s]
            halo = tile
            for j, i in enumerate(CROSS_Y[s]):
                cx, _, cz = VELOCITIES[i]
                if cx:
                    corner = xy_in[step, side(-cx), s]
                    shifted = pltpu.roll(tile, PY - 1 if cx == 1 else 1, axis=1)
                    corner = pltpu.roll(corner, PX - 1 if cx == 1 else PY - PX + 1, axis=1)
                    shifted = jnp.where(
                        lane == j * PX + (PX - 1 if cx == 1 else 0), corner, shifted
                    )
                elif cz:
                    corner = yz_in[step, s, side(-cz)]
                    shifted = jnp.where(row == (0 if cz == 1 else PZ - 1), corner, tile)
                    shifted = pltpu.roll(shifted, PZ - 1 if cz == 1 else 1, axis=0)
                else:
                    continue
                halo = jnp.where(
                    jnp.logical_and(lane >= j * PX, lane < (j + 1) * PX), shifted, halo
                )
            halos.append(halo)
        return halos

    def advance(step, halos, x):
        pulled = []
        for i, (cx, cy, cz) in enumerate(VELOCITIES):
            value = field[step, i, plane(x + (1 + cx)), :]
            if cz:
                value = pltpu.roll(value, PZ - 1 if cz == 1 else 1, axis=0)
            if cy:
                s = 0 if cy == 1 else 1
                at = CROSS_Y[s].index(i) * PX + x
                edge = PY - 1 if cy == 1 else 0
                value = pltpu.roll(value, PY - 1 if cy == 1 else 1, axis=1)
                column = pltpu.roll(halos[s], lax.rem(edge + PY - at, PY), axis=1)
                value = jnp.where(lane == edge, column, value)
            pulled.append(value)
        here_rows = plane(x)
        u = [vel[d, here_rows, :] for d in range(3)]
        new, gain = collide(
            pulled, rho[here_rows, :], u, por[here_rows, :], node[here_rows, :]
        )
        sens[here_rows, :] = sens[here_rows, :] + gain
        return new

    blank = (jnp.zeros((PZ, PY), jnp.float32),) * 2
    loads[0].wait()
    tiles = lax.fori_loop(
        0,
        PX,
        lambda x, t: columns(lambda i: field[0, i, plane(x + 1), :], x, t),
        blank,
    )
    first = exchange(0, tiles)
    for copy in loads[1:]:
        copy.wait()
    halos = insert(0, first)

    def first_step(x, t):
        new = advance(0, halos, x)
        for i in range(19):
            field[1, i, plane(x + 1), :] = new[i]
        return columns(lambda i: new[i], x, t)

    tiles = lax.fori_loop(0, PX, first_step, blank)
    second = exchange(1, tiles)
    halos = insert(1, second)

    stores = []
    parts = 4
    for part in range(parts):

        def second_step(x, _):
            new = advance(1, halos, x)
            for i in range(19):
                result[i, plane(x), :] = new[i]
            return _

        lax.fori_loop(part * PX // parts, (part + 1) * PX // parts, second_step, 0)
        span = pl.ds(part * ROWS // parts, ROWS // parts)
        stores.append(
            pltpu.make_async_copy(
                result.at[:, span, :], out_hbm.at[:, span, :], store_sem.at[part]
            )
        )
        stores[-1].start()
    stores.append(pltpu.make_async_copy(sens, out_sens_hbm, store_sem.at[parts]))
    stores[-1].start()
    for copies in (first, second):
        for route in ROUTES:
            copies[route].wait_send()
    for copy in stores:
        copy.wait()


def shards(adjoint, density, velocity, porosity, node_type, sensitivity_in):
    f32 = jnp.float32
    dma = pltpu.SemaphoreType.DMA
    anywhere = pl.BlockSpec(memory_space=pl.ANY)
    out, sens = pl.pallas_call(
        lattice_kernel,
        out_shape=(
            jax.ShapeDtypeStruct((19, ROWS, PY), f32),
            jax.ShapeDtypeStruct((ROWS, PY), f32),
        ),
        in_specs=[anywhere] * 6,
        out_specs=(anywhere, anywhere),
        scratch_shapes=[
            pltpu.VMEM((2, 19, ROWS + 2 * PZ, PY), f32),
            pltpu.VMEM((ROWS, PY), f32),
            pltpu.VMEM((3, ROWS, PY), f32),
            pltpu.VMEM((ROWS, PY), f32),
            pltpu.VMEM((ROWS, PY), jnp.int32),
            pltpu.VMEM((ROWS, PY), f32),
            pltpu.VMEM((19, ROWS, PY), f32),
            pltpu.VMEM((2, 2, 5, PZ, PY), f32),
            pltpu.VMEM((2, 2, PZ, PY), f32),
            pltpu.VMEM((2, 2, 5, PX, PY), f32),
            pltpu.VMEM((2, 2, 5, PZ, PY), f32),
            pltpu.VMEM((2, 2, PZ, PY), f32),
            pltpu.VMEM((2, 2, 5, PX, PY), f32),
            pltpu.VMEM((2, 2, 2, PZ, PY), f32),
            pltpu.VMEM((2, 2, 2, PZ, PY), f32),
            pltpu.VMEM((2, 2, 2, PZ, PY), f32),
            dma((6,)),
            dma((5,)),
            dma((2, len(ROUTES))),
            dma((2, len(ROUTES))),
        ],
        compiler_params=pltpu.CompilerParams(
            collective_id=0, has_side_effects=True, vmem_limit_bytes=32 * 1024 * 1024
        ),
    )(
        adjoint.reshape(19, ROWS, PY),
        density.reshape(ROWS, PY),
        velocity.reshape(3, ROWS, PY),
        porosity.reshape(ROWS, PY),
        node_type.reshape(ROWS, PY),
        sensitivity_in.reshape(ROWS, PY),
    )
    return out.reshape(19, PX, PZ, PY), sens.reshape(PX, PZ, PY)


def solution(mesh):
    cells = P("gx", "gz", "gy")
    many = P(None, "gx", "gz", "gy")
    return jax.shard_map(
        shards,
        mesh=mesh,
        in_specs=(many, cells, many, cells, cells, cells),
        out_specs=(many, cells),
        check_vma=False,
    )
```

```python
import functools

import jax
import jax.numpy as jnp
from jax import lax
from jax.experimental import pallas as pl
from jax.experimental.pallas import tpu as pltpu
from jax.sharding import PartitionSpec as P

AXES = ("gx", "gy", "gz")
PX, PZ, PY = 16, 8, 128
ROWS = PX * PZ

VELOCITIES = [
    (0, 0, 0),
    (1, 0, 0),
    (-1, 0, 0),
    (0, 1, 0),
    (0, -1, 0),
    (0, 0, 1),
    (0, 0, -1),
    (1, 1, 0),
    (-1, -1, 0),
    (1, -1, 0),
    (-1, 1, 0),
    (1, 0, 1),
    (-1, 0, -1),
    (1, 0, -1),
    (-1, 0, 1),
    (0, 1, 1),
    (0, -1, -1),
    (0, 1, -1),
    (0, -1, 1),
]
CROSS = [[[i for i, c in enumerate(VELOCITIES) if c[a] == s] for s in (1, -1)] for a in range(3)]
CROSS_X, CROSS_Y, CROSS_Z = CROSS
FACES_X = [(-1, 0, 0), (1, 0, 0)]
FACES_Y = [(0, -1, 0), (0, 1, 0)]
FACES_Z = [(0, 0, -1), (0, 0, 1)]
EDGES_XY = [(a, b, 0) for a in (-1, 1) for b in (-1, 1)]
EDGES_YZ = [(0, a, b) for a in (-1, 1) for b in (-1, 1)]
EDGES_XZ = [(a, 0, b) for a in (-1, 1) for b in (-1, 1)]
ROUTES = EDGES_XZ + EDGES_XY + EDGES_YZ + FACES_Y + FACES_X + FACES_Z


def side(sign):
    return (sign + 1) // 2


def collide(p, rho, u, g, node):
    ux, uy, uz = u
    e = [p[i] + p[i + 1] for i in range(1, 19, 2)]
    o = [p[i] - p[i + 1] for i in range(1, 19, 2)]
    sxy, sxz, syz = e[3] + e[4], e[5] + e[6], e[7] + e[8]
    dxy, dxz, dyz = e[3] - e[4], e[5] - e[6], e[7] - e[8]
    sx = 2.0 * e[0] + (sxy + sxz)
    sy = 2.0 * e[1] + (sxy + syz)
    sz = 2.0 * e[2] + (sxz + syz)
    trace = sx + sy + sz
    h36 = 12.0 * p[0] + (trace - (sxy + sxz + syz))
    third = h36 * (1.0 / 3.0)
    mxx, myy, mzz = sx - third, sy - third, sz - third
    hcx = 2.0 * o[0] + ((o[3] + o[4]) + (o[5] + o[6]))
    hcy = 2.0 * o[1] + ((o[3] - o[4]) + (o[7] + o[8]))
    hcz = 2.0 * o[2] + ((o[5] - o[6]) + (o[7] - o[8]))
    nx = mxx * ux + dxy * uy + dxz * uz
    ny = dxy * ux + myy * uy + dyz * uz
    nz = dxz * ux + dyz * uy + mzz * uz
    q = ux * nx + uy * ny + uz * nz
    first = ux * hcx + uy * hcy + uz * hcz
    g4 = 0.4 * g
    b = g4 * g
    a = g * (1.0 / 12.0) + (1.0 / 60.0)
    gain = rho * (first * (1.0 / 12.0) + g4 * q)
    inlet = node == 1
    wall = node == 2
    vx = a * hcx + b * nx + jnp.where(inlet, 1.0, 0.0)
    vy = a * hcy + b * ny
    vz = a * hcz + b * nz
    base = h36 * (1.1 / 36.0) + trace * (1.0 / 120.0) - (0.5 * b) * q
    ex, ey, ez = -0.025 * mxx, -0.025 * myy, -0.025 * mzz
    bx, by = base + ex, base + ey
    bz = base + ez
    bxy, bxz, byz = bx + ey, bx + ez, by + ez
    wxy, wxz, wyz = 0.05 * dxy, 0.05 * dxz, 0.05 * dyz
    even = [bx, by, bz, bxy - wxy, bxy + wxy, bxz - wxz, bxz + wxz, byz - wyz, byz + wyz]
    odd = [vx, vy, vz, vx + vy, vx - vy, vx + vz, vx - vz, vy + vz, vy - vz]
    new = [jnp.where(wall, p[0], base - 0.4 * p[0])]
    for k in range(9):
        up = even[k] - 0.2 * e[k]
        down = odd[k] - 0.1 * o[k]
        new.append(jnp.where(wall, p[2 * k + 2], up + down))
        new.append(jnp.where(wall, p[2 * k + 1], up - down))
    return new, jnp.where(wall, 0.0, gain)


def lattice_kernel(
    adj_hbm,
    rho_hbm,
    vel_hbm,
    por_hbm,
    node_hbm,
    sens_hbm,
    result,
    sens,
    field,
    rho,
    vel,
    por,
    node,
    x_out,
    y_out,
    z_out,
    x_in,
    y_in,
    z_in,
    xy_in,
    yz_in,
    xz_in,
    load_sem,
    send_sem,
    recv_sem,
):
    here = [lax.axis_index(a) for a in AXES]
    size = [lax.axis_size(a) for a in AXES]

    def device(route):
        return tuple(lax.rem(h + (d + n), n) if d else h for h, d, n in zip(here, route, size))

    barrier = pltpu.get_barrier_semaphore()
    for route in ROUTES:
        pl.semaphore_signal(
            barrier, inc=1, device_id=device(route), device_id_type=pl.DeviceIdType.MESH
        )
    own = pl.ds(PZ, ROWS)
    loads = [
        pltpu.make_async_copy(src, dst, load_sem.at[k])
        for k, (src, dst) in enumerate(
            [
                (adj_hbm, field.at[0, :, own, :]),
                (rho_hbm, rho),
                (vel_hbm, vel),
                (por_hbm, por),
                (node_hbm, node),
                (sens_hbm, sens),
            ]
        )
    ]
    for copy in loads:
        copy.start()

    lane = lax.broadcasted_iota(jnp.int32, (PZ, PY), 1)
    row = lax.broadcasted_iota(jnp.int32, (PZ, PY), 0)

    def plane(x):
        return pl.ds(pl.multiple_of(x * PZ, PZ), PZ)

    def columns(values, x, tiles):
        made = []
        for s in range(2):
            tile = tiles[s]
            for j, i in enumerate(CROSS_Y[s]):
                at = x + j * PX
                turned = pltpu.roll(values(i), at if s == 0 else at + 1, axis=1)
                tile = jnp.where(lane == at, turned, tile)
            made.append(tile)
        return tuple(made)

    def exchange(step, tiles):
        for s in range(2):
            y_out[step, s] = tiles[s]
            for j, i in enumerate(CROSS_Z[s]):
                z_out[step, s, j] = field[step, i, pl.ds(PZ + s * (PZ - 1), PX, stride=PZ), :]
            for j, i in enumerate(CROSS_X[s]):
                x_out[step, s, j] = field[step, i, pl.ds(PZ * (PX if s else 1), PZ), :]
        if step == 0:
            pl.semaphore_wait(barrier, len(ROUTES))
        copies = {}
        for k, route in enumerate(ROUTES):
            dx, dy, dz = route
            if route in FACES_X:
                src, dst = x_out.at[step, side(dx)], x_in.at[step, side(dx)]
            elif route in FACES_Z:
                src, dst = z_out.at[step, side(dz)], z_in.at[step, side(dz)]
            elif route in FACES_Y:
                src, dst = y_out.at[step, side(dy)], y_in.at[step, side(dy)]
            elif route in EDGES_XY:
                src, dst = y_out.at[step, side(dy)], xy_in.at[step, side(dx), side(dy)]
            elif route in EDGES_YZ:
                src, dst = y_out.at[step, side(dy)], yz_in.at[step, side(dy), side(dz)]
            else:
                j = CROSS_Z[side(dz)].index(VELOCITIES.index((-dx, 0, -dz)))
                src = z_out.at[step, side(dz), j, pl.ds(side(dx) * (PX - 8), 8), :]
                dst = xz_in.at[step, side(dx), side(dz)]
            copy = pltpu.make_async_remote_copy(
                src_ref=src,
                dst_ref=dst,
                send_sem=send_sem.at[step, k],
                recv_sem=recv_sem.at[step, k],
                device_id=device(route),
                device_id_type=pl.DeviceIdType.MESH,
            )
            copy.start()
            copies[route] = copy
        return copies

    def insert(step, copies):
        for route in ROUTES:
            copies[route].wait_recv()
        for s in range(2):
            for j, i in enumerate(CROSS_X[s]):
                field[step, i, pl.ds(0 if s else PZ * (PX + 1), PZ), :] = x_in[step, s, j]
            for j, i in enumerate(CROSS_Z[s]):
                field[step, i, pl.ds(PZ + s * (PZ - 1), PX, stride=PZ), :] = z_in[step, s, j]
        for dx, _, dz in EDGES_XZ:
            i = VELOCITIES.index((-dx, 0, -dz))
            at = (0 if dx == 1 else PZ * (PX + 1)) + side(dz) * (PZ - 1)
            field[step, i, pl.ds(at, 1), :] = xz_in[
                step, side(dx), side(dz), pl.ds(side(dx) * (PZ - 1), 1), :
            ]
        halos = []
        for s in range(2):
            tile = y_in[step, s]
            halo = tile
            for j, i in enumerate(CROSS_Y[s]):
                cx, _, cz = VELOCITIES[i]
                if cx:
                    corner = xy_in[step, side(-cx), s]
                    shifted = pltpu.roll(tile, PY - 1 if cx == 1 else 1, axis=1)
                    corner = pltpu.roll(corner, PX - 1 if cx == 1 else PY - PX + 1, axis=1)
                    shifted = jnp.where(
                        lane == j * PX + (PX - 1 if cx == 1 else 0), corner, shifted
                    )
                elif cz:
                    corner = yz_in[step, s, side(-cz)]
                    shifted = jnp.where(row == (0 if cz == 1 else PZ - 1), corner, tile)
                    shifted = pltpu.roll(shifted, PZ - 1 if cz == 1 else 1, axis=0)
                else:
                    continue
                halo = jnp.where(
                    jnp.logical_and(lane >= j * PX, lane < (j + 1) * PX), shifted, halo
                )
            halos.append(halo)
        return halos

    def advance(step, halos, x):
        pulled = []
        for i, (cx, cy, cz) in enumerate(VELOCITIES):
            value = field[step, i, plane(x + (1 + cx)), :]
            if cz:
                value = pltpu.roll(value, PZ - 1 if cz == 1 else 1, axis=0)
            if cy:
                s = 0 if cy == 1 else 1
                at = CROSS_Y[s].index(i) * PX + x
                edge = PY - 1 if cy == 1 else 0
                value = pltpu.roll(value, PY - 1 if cy == 1 else 1, axis=1)
                column = pltpu.roll(halos[s], lax.rem(edge + PY - at, PY), axis=1)
                value = jnp.where(lane == edge, column, value)
            pulled.append(value)
        here_rows = plane(x)
        u = [vel[d, here_rows, :] for d in range(3)]
        new, gain = collide(
            pulled, rho[here_rows, :], u, por[here_rows, :], node[here_rows, :]
        )
        sens[here_rows, :] = sens[here_rows, :] + gain
        return new

    blank = (jnp.zeros((PZ, PY), jnp.float32),) * 2
    loads[0].wait()
    tiles = lax.fori_loop(
        0,
        PX,
        lambda x, t: columns(lambda i: field[0, i, plane(x + 1), :], x, t),
        blank,
        unroll=4,
    )
    first = exchange(0, tiles)
    for copy in loads[1:]:
        copy.wait()
    halos = insert(0, first)

    def first_step(x, t):
        new = advance(0, halos, x)
        for i in range(19):
            field[1, i, plane(x + 1), :] = new[i]
        return columns(lambda i: new[i], x, t)

    tiles = lax.fori_loop(0, PX, first_step, blank, unroll=4)
    second = exchange(1, tiles)
    halos = insert(1, second)

    def second_step(x, carry):
        new = advance(1, halos, x)
        for i in range(19):
            result[i, plane(x), :] = new[i]
        return carry

    lax.fori_loop(0, PX, second_step, 0, unroll=4)
    for copies in (first, second):
        for route in ROUTES:
            copies[route].wait_send()


def shards(adjoint, density, velocity, porosity, node_type, sensitivity_in):
    f32 = jnp.float32
    dma = pltpu.SemaphoreType.DMA
    anywhere = pl.BlockSpec(memory_space=pl.ANY)
    out, sens = pl.pallas_call(
        lattice_kernel,
        out_shape=(
            pltpu.VMEM((19, ROWS, PY), f32),
            pltpu.VMEM((ROWS, PY), f32),
        ),
        in_specs=[anywhere] * 6,
        out_specs=(pl.BlockSpec(memory_space=pltpu.VMEM),) * 2,
        scratch_shapes=[
            pltpu.VMEM((2, 19, ROWS + 2 * PZ, PY), f32),
            pltpu.VMEM((ROWS, PY), f32),
            pltpu.VMEM((3, ROWS, PY), f32),
            pltpu.VMEM((ROWS, PY), f32),
            pltpu.VMEM((ROWS, PY), jnp.int32),
            pltpu.VMEM((2, 2, 5, PZ, PY), f32),
            pltpu.VMEM((2, 2, PZ, PY), f32),
            pltpu.VMEM((2, 2, 5, PX, PY), f32),
            pltpu.VMEM((2, 2, 5, PZ, PY), f32),
            pltpu.VMEM((2, 2, PZ, PY), f32),
            pltpu.VMEM((2, 2, 5, PX, PY), f32),
            pltpu.VMEM((2, 2, 2, PZ, PY), f32),
            pltpu.VMEM((2, 2, 2, PZ, PY), f32),
            pltpu.VMEM((2, 2, 2, PZ, PY), f32),
            dma((6,)),
            dma((2, len(ROUTES))),
            dma((2, len(ROUTES))),
        ],
        compiler_params=pltpu.CompilerParams(
            collective_id=0, has_side_effects=True, vmem_limit_bytes=56 * 1024 * 1024
        ),
    )(
        adjoint.reshape(19, ROWS, PY),
        density.reshape(ROWS, PY),
        velocity.reshape(3, ROWS, PY),
        porosity.reshape(ROWS, PY),
        node_type.reshape(ROWS, PY),
        sensitivity_in.reshape(ROWS, PY),
    )
    return out.reshape(19, PX, PZ, PY), sens.reshape(PX, PZ, PY)


def solution(mesh):
    cells = P("gx", "gz", "gy")
    many = P(None, "gx", "gz", "gy")
    return jax.shard_map(
        shards,
        mesh=mesh,
        in_specs=(many, cells, many, cells, cells, cells),
        out_specs=(many, cells),
        check_vma=False,
    )
```

```python
import functools

import jax
import jax.numpy as jnp
from jax import lax
from jax.experimental import pallas as pl
from jax.experimental.pallas import tpu as pltpu
from jax.sharding import PartitionSpec as P

AXES = ("gx", "gy", "gz")
PX, PZ, PY = 16, 8, 128
ROWS = PX * PZ

VELOCITIES = [
    (0, 0, 0),
    (1, 0, 0),
    (-1, 0, 0),
    (0, 1, 0),
    (0, -1, 0),
    (0, 0, 1),
    (0, 0, -1),
    (1, 1, 0),
    (-1, -1, 0),
    (1, -1, 0),
    (-1, 1, 0),
    (1, 0, 1),
    (-1, 0, -1),
    (1, 0, -1),
    (-1, 0, 1),
    (0, 1, 1),
    (0, -1, -1),
    (0, 1, -1),
    (0, -1, 1),
]
CROSS = [[[i for i, c in enumerate(VELOCITIES) if c[a] == s] for s in (1, -1)] for a in range(3)]
CROSS_X, CROSS_Y, CROSS_Z = CROSS
FACES_X = [(-1, 0, 0), (1, 0, 0)]
FACES_Y = [(0, -1, 0), (0, 1, 0)]
FACES_Z = [(0, 0, -1), (0, 0, 1)]
EDGES_XY = [(a, b, 0) for a in (-1, 1) for b in (-1, 1)]
EDGES_YZ = [(0, a, b) for a in (-1, 1) for b in (-1, 1)]
EDGES_XZ = [(a, 0, b) for a in (-1, 1) for b in (-1, 1)]
ROUTES = EDGES_XZ + EDGES_XY + FACES_Z + EDGES_YZ + FACES_Y + FACES_X


def side(sign):
    return (sign + 1) // 2


def collide(p, rho, u, g, node):
    ux, uy, uz = u
    e = [p[i] + p[i + 1] for i in range(1, 19, 2)]
    o = [p[i] - p[i + 1] for i in range(1, 19, 2)]
    sxy, sxz, syz = e[3] + e[4], e[5] + e[6], e[7] + e[8]
    dxy, dxz, dyz = e[3] - e[4], e[5] - e[6], e[7] - e[8]
    sx = 2.0 * e[0] + (sxy + sxz)
    sy = 2.0 * e[1] + (sxy + syz)
    sz = 2.0 * e[2] + (sxz + syz)
    trace = sx + sy + sz
    h36 = 12.0 * p[0] + (trace - (sxy + sxz + syz))
    third = h36 * (1.0 / 3.0)
    mxx, myy, mzz = sx - third, sy - third, sz - third
    hcx = 2.0 * o[0] + ((o[3] + o[4]) + (o[5] + o[6]))
    hcy = 2.0 * o[1] + ((o[3] - o[4]) + (o[7] + o[8]))
    hcz = 2.0 * o[2] + ((o[5] - o[6]) + (o[7] - o[8]))
    nx = mxx * ux + dxy * uy + dxz * uz
    ny = dxy * ux + myy * uy + dyz * uz
    nz = dxz * ux + dyz * uy + mzz * uz
    q = ux * nx + uy * ny + uz * nz
    first = ux * hcx + uy * hcy + uz * hcz
    g4 = 0.4 * g
    b = g4 * g
    a = g * (1.0 / 12.0) + (1.0 / 60.0)
    gain = rho * (first * (1.0 / 12.0) + g4 * q)
    inlet = node == 1
    wall = node == 2
    vx = a * hcx + b * nx + jnp.where(inlet, 1.0, 0.0)
    vy = a * hcy + b * ny
    vz = a * hcz + b * nz
    base = h36 * (1.1 / 36.0) + trace * (1.0 / 120.0) - (0.5 * b) * q
    ex, ey, ez = -0.025 * mxx, -0.025 * myy, -0.025 * mzz
    bx, by = base + ex, base + ey
    bz = base + ez
    bxy, bxz, byz = bx + ey, bx + ez, by + ez
    wxy, wxz, wyz = 0.05 * dxy, 0.05 * dxz, 0.05 * dyz
    even = [bx, by, bz, bxy - wxy, bxy + wxy, bxz - wxz, bxz + wxz, byz - wyz, byz + wyz]
    odd = [vx, vy, vz, vx + vy, vx - vy, vx + vz, vx - vz, vy + vz, vy - vz]
    new = [jnp.where(wall, p[0], base - 0.4 * p[0])]
    for k in range(9):
        up = even[k] - 0.2 * e[k]
        down = odd[k] - 0.1 * o[k]
        new.append(jnp.where(wall, p[2 * k + 2], up + down))
        new.append(jnp.where(wall, p[2 * k + 1], up - down))
    return new, jnp.where(wall, 0.0, gain)


def lattice_kernel(
    adj_hbm,
    rho_hbm,
    vel_hbm,
    por_hbm,
    node_hbm,
    sens_hbm,
    result,
    sens,
    field,
    rho,
    vel,
    por,
    node,
    x_out,
    y_out,
    z_out,
    x_in,
    y_in,
    z_in,
    xy_in,
    yz_in,
    xz_in,
    load_sem,
    send_sem,
    recv_sem,
):
    here = [lax.axis_index(a) for a in AXES]
    size = [lax.axis_size(a) for a in AXES]

    def device(route):
        return tuple(lax.rem(h + (d + n), n) if d else h for h, d, n in zip(here, route, size))

    barrier = pltpu.get_barrier_semaphore()
    for route in ROUTES:
        pl.semaphore_signal(
            barrier, inc=1, device_id=device(route), device_id_type=pl.DeviceIdType.MESH
        )
    own = pl.ds(PZ, ROWS)
    loads = [
        pltpu.make_async_copy(src, dst, load_sem.at[k])
        for k, (src, dst) in enumerate(
            [
                (adj_hbm, field.at[0, :, own, :]),
                (rho_hbm, rho),
                (vel_hbm, vel),
                (por_hbm, por),
                (node_hbm, node),
                (sens_hbm, sens),
            ]
        )
    ]
    for copy in loads:
        copy.start()

    lane = lax.broadcasted_iota(jnp.int32, (PZ, PY), 1)
    row = lax.broadcasted_iota(jnp.int32, (PZ, PY), 0)

    def plane(x):
        if isinstance(x, int):
            return pl.ds(x * PZ, PZ)
        return pl.ds(pl.multiple_of(x * PZ, PZ), PZ)

    def pack_columns(step, x, tiles):
        made = []
        for s in range(2):
            tile = tiles[s]
            for j, i in enumerate(CROSS_Y[s]):
                at = x + j * PX
                value = field[step, i, plane(x + 1), :]
                turned = pltpu.roll(value, at if s == 0 else at + 1, axis=1)
                tile = jnp.where(lane == at, turned, tile)
            made.append(tile)
        return tuple(made)

    def put_column(step, i, x, tile, at):
        edge = 0 if VELOCITIES[i][1] == 1 else PY - 1
        shift = (edge - at) % PY if isinstance(at, int) else edge + PY - at
        column = pltpu.roll(tile, shift, axis=1)
        field[step, i, plane(x + 1), :] = jnp.where(
            lane == edge, column, field[step, i, plane(x + 1), :]
        )

    def exchange(step, tiles):
        for s in range(2):
            y_out[step, s] = tiles[s]
            for j, i in enumerate(CROSS_Z[s]):
                z_out[step, s, j] = field[step, i, pl.ds(PZ + s * (PZ - 1), PX, stride=PZ), :]
            for j, i in enumerate(CROSS_X[s]):
                x_out[step, s, j] = field[step, i, pl.ds(PZ * (PX if s else 1), PZ), :]
        if step == 0:
            pl.semaphore_wait(barrier, len(ROUTES))
        copies = {}
        for k, route in enumerate(ROUTES):
            dx, dy, dz = route
            if route in FACES_X:
                src, dst = x_out.at[step, side(dx)], x_in.at[step, side(dx)]
            elif route in FACES_Z:
                src, dst = z_out.at[step, side(dz)], z_in.at[step, side(dz)]
            elif route in FACES_Y:
                src, dst = y_out.at[step, side(dy)], y_in.at[step, side(dy)]
            elif route in EDGES_XY:
                src, dst = y_out.at[step, side(dy)], xy_in.at[step, side(dx), side(dy)]
            elif route in EDGES_YZ:
                src, dst = y_out.at[step, side(dy)], yz_in.at[step, side(dy), side(dz)]
            else:
                j = CROSS_Z[side(dz)].index(VELOCITIES.index((-dx, 0, -dz)))
                src = z_out.at[step, side(dz), j, pl.ds(side(dx) * (PX - 8), 8), :]
                dst = xz_in.at[step, side(dx), side(dz)]
            copy = pltpu.make_async_remote_copy(
                src_ref=src,
                dst_ref=dst,
                send_sem=send_sem.at[step, k],
                recv_sem=recv_sem.at[step, k],
                device_id=device(route),
                device_id_type=pl.DeviceIdType.MESH,
            )
            copy.start()
            copies[route] = copy
        return copies

    def insert_y(step, copies):
        for route in FACES_Y + EDGES_YZ:
            copies[route].wait_recv()
        tiles = {}
        for s in range(2):
            for i in CROSS_Y[s]:
                cz = VELOCITIES[i][2]
                tiles[i] = y_in[step, s]
                if cz:
                    tiles[i] = jnp.where(
                        row == (0 if cz == 1 else PZ - 1), yz_in[step, s, side(-cz)], tiles[i]
                    )

        def body(x, carry):
            for s in range(2):
                for j, i in enumerate(CROSS_Y[s]):
                    put_column(step, i, x, tiles[i], x + j * PX)
            return carry

        lax.fori_loop(0, PX, body, 0, unroll=4)

    def insert_z(step, copies):
        for route in FACES_Z:
            copies[route].wait_recv()
        wide = lax.broadcasted_iota(jnp.int32, (PX, PY), 1)
        for s in range(2):
            for j, i in enumerate(CROSS_Z[s]):
                rows = pl.ds(PZ + s * (PZ - 1), PX, stride=PZ)
                value = z_in[step, s, j]
                cy = VELOCITIES[i][1]
                if cy:
                    value = jnp.where(
                        wide == (0 if cy == 1 else PY - 1), field[step, i, rows, :], value
                    )
                field[step, i, rows, :] = value

    def insert_x(step, copies):
        for route in FACES_X + EDGES_XY + EDGES_XZ:
            copies[route].wait_recv()
        for s in range(2):
            for j, i in enumerate(CROSS_X[s]):
                field[step, i, plane(0 if s else PX + 1), :] = x_in[step, s, j]
        for dx, _, dz in EDGES_XZ:
            i = VELOCITIES.index((-dx, 0, -dz))
            at = (0 if dx == 1 else PZ * (PX + 1)) + side(dz) * (PZ - 1)
            field[step, i, pl.ds(at, 1), :] = xz_in[
                step, side(dx), side(dz), pl.ds(side(dx) * (PZ - 1), 1), :
            ]
        for dx, dy, _ in EDGES_XY:
            i = VELOCITIES.index((-dx, -dy, 0))
            at = CROSS_Y[side(dy)].index(i) * PX + (PX - 1 if dx == 1 else 0)
            put_column(step, i, -1 if dx == 1 else PX, xy_in[step, side(dx), side(dy)], at)

    def advance(step, x):
        pulled = []
        for i, (cx, cy, cz) in enumerate(VELOCITIES):
            value = field[step, i, plane(x + (1 + cx)), :]
            if cz:
                value = pltpu.roll(value, PZ - 1 if cz == 1 else 1, axis=0)
            if cy:
                value = pltpu.roll(value, PY - 1 if cy == 1 else 1, axis=1)
            pulled.append(value)
        here_rows = plane(x)
        u = [vel[d, here_rows, :] for d in range(3)]
        new, gain = collide(
            pulled, rho[here_rows, :], u, por[here_rows, :], node[here_rows, :]
        )
        sens[here_rows, :] = sens[here_rows, :] + gain
        return new

    def first_step(x, carry):
        new = advance(0, x)
        for i in range(19):
            field[1, i, plane(x + 1), :] = new[i]
        return carry

    def second_step(x, carry):
        new = advance(1, x)
        for i in range(19):
            result[i, plane(x), :] = new[i]
        return carry

    def pack(step, low, high, tiles):
        return lax.fori_loop(
            low, high, lambda x, t: pack_columns(step, x, t), tiles, unroll=high - low
        )

    blank = (jnp.zeros((PZ, PY), jnp.float32),) * 2
    loads[0].wait()
    tiles = pack(0, 0, PX, blank)
    first = exchange(0, tiles)
    for copy in loads[1:]:
        copy.wait()
    insert_y(0, first)
    insert_z(0, first)
    lax.fori_loop(1, PX - 1, first_step, 0, unroll=7)
    tiles = pack(1, 1, PX - 1, blank)
    insert_x(0, first)
    for x in (0, PX - 1):
        first_step(x, 0)
        tiles = pack_columns(1, x, tiles)
    second = exchange(1, tiles)
    insert_y(1, second)
    insert_z(1, second)
    lax.fori_loop(1, PX - 1, second_step, 0, unroll=7)
    insert_x(1, second)
    for x in (0, PX - 1):
        second_step(x, 0)
    for copies in (first, second):
        for route in ROUTES:
            copies[route].wait_send()


def store_kernel(result, sens, out_hbm, out_sens_hbm, sem):
    copies = [
        pltpu.make_async_copy(result, out_hbm, sem.at[0]),
        pltpu.make_async_copy(sens, out_sens_hbm, sem.at[1]),
    ]
    for copy in copies:
        copy.start()
    for copy in copies:
        copy.wait()


def shards(adjoint, density, velocity, porosity, node_type, sensitivity_in):
    f32 = jnp.float32
    dma = pltpu.SemaphoreType.DMA
    anywhere = pl.BlockSpec(memory_space=pl.ANY)
    made = pl.pallas_call(
        lattice_kernel,
        out_shape=(
            pltpu.VMEM((19, ROWS, PY), f32),
            pltpu.VMEM((ROWS, PY), f32),
        ),
        in_specs=[anywhere] * 6,
        out_specs=(pl.BlockSpec(memory_space=pltpu.VMEM),) * 2,
        scratch_shapes=[
            pltpu.VMEM((2, 19, ROWS + 2 * PZ, PY), f32),
            pltpu.VMEM((ROWS, PY), f32),
            pltpu.VMEM((3, ROWS, PY), f32),
            pltpu.VMEM((ROWS, PY), f32),
            pltpu.VMEM((ROWS, PY), jnp.int32),
            pltpu.VMEM((2, 2, 5, PZ, PY), f32),
            pltpu.VMEM((2, 2, PZ, PY), f32),
            pltpu.VMEM((2, 2, 5, PX, PY), f32),
            pltpu.VMEM((2, 2, 5, PZ, PY), f32),
            pltpu.VMEM((2, 2, PZ, PY), f32),
            pltpu.VMEM((2, 2, 5, PX, PY), f32),
            pltpu.VMEM((2, 2, 2, PZ, PY), f32),
            pltpu.VMEM((2, 2, 2, PZ, PY), f32),
            pltpu.VMEM((2, 2, 2, PZ, PY), f32),
            dma((6,)),
            dma((2, len(ROUTES))),
            dma((2, len(ROUTES))),
        ],
        compiler_params=pltpu.CompilerParams(
            collective_id=0, has_side_effects=True, vmem_limit_bytes=56 * 1024 * 1024
        ),
    )(
        adjoint.reshape(19, ROWS, PY),
        density.reshape(ROWS, PY),
        velocity.reshape(3, ROWS, PY),
        porosity.reshape(ROWS, PY),
        node_type.reshape(ROWS, PY),
        sensitivity_in.reshape(ROWS, PY),
    )
    out, sens = pl.pallas_call(
        store_kernel,
        out_shape=(
            jax.ShapeDtypeStruct((19, ROWS, PY), f32),
            jax.ShapeDtypeStruct((ROWS, PY), f32),
        ),
        in_specs=[anywhere] * 2,
        out_specs=(anywhere, anywhere),
        scratch_shapes=[dma((2,))],
        compiler_params=pltpu.CompilerParams(vmem_limit_bytes=1024 * 1024),
    )(*made)
    return out.reshape(19, PX, PZ, PY), sens.reshape(PX, PZ, PY)


def solution(mesh):
    cells = P("gx", "gz", "gy")
    many = P(None, "gx", "gz", "gy")
    return jax.shard_map(
        shards,
        mesh=mesh,
        in_specs=(many, cells, many, cells, cells, cells),
        out_specs=(many, cells),
        check_vma=False,
    )
```

```python
import functools

import jax
import jax.numpy as jnp
from jax import lax
from jax.experimental import pallas as pl
from jax.experimental.pallas import tpu as pltpu
from jax.sharding import PartitionSpec as P

AXES = ("gx", "gy", "gz")
PX, PZ, PY = 16, 8, 128
ROWS = PX * PZ

VELOCITIES = [
    (0, 0, 0),
    (1, 0, 0),
    (-1, 0, 0),
    (0, 1, 0),
    (0, -1, 0),
    (0, 0, 1),
    (0, 0, -1),
    (1, 1, 0),
    (-1, -1, 0),
    (1, -1, 0),
    (-1, 1, 0),
    (1, 0, 1),
    (-1, 0, -1),
    (1, 0, -1),
    (-1, 0, 1),
    (0, 1, 1),
    (0, -1, -1),
    (0, 1, -1),
    (0, -1, 1),
]
CROSS = [[[i for i, c in enumerate(VELOCITIES) if c[a] == s] for s in (1, -1)] for a in range(3)]
CROSS_X, CROSS_Y, CROSS_Z = CROSS
FACES_X = [(-1, 0, 0), (1, 0, 0)]
FACES_Y = [(0, -1, 0), (0, 1, 0)]
FACES_Z = [(0, 0, -1), (0, 0, 1)]
EDGES_XY = [(a, b, 0) for a in (-1, 1) for b in (-1, 1)]
EDGES_YZ = [(0, a, b) for a in (-1, 1) for b in (-1, 1)]
EDGES_XZ = [(a, 0, b) for a in (-1, 1) for b in (-1, 1)]
FAR = EDGES_XZ + EDGES_XY + FACES_X
NEAR = FACES_Z + EDGES_YZ + FACES_Y
ROUTES = FAR + NEAR


def side(sign):
    return (sign + 1) // 2


def collide(p, rho, u, g, node):
    ux, uy, uz = u
    e = [p[i] + p[i + 1] for i in range(1, 19, 2)]
    o = [p[i] - p[i + 1] for i in range(1, 19, 2)]
    sxy, sxz, syz = e[3] + e[4], e[5] + e[6], e[7] + e[8]
    dxy, dxz, dyz = e[3] - e[4], e[5] - e[6], e[7] - e[8]
    sx = 2.0 * e[0] + (sxy + sxz)
    sy = 2.0 * e[1] + (sxy + syz)
    sz = 2.0 * e[2] + (sxz + syz)
    trace = sx + sy + sz
    h36 = 12.0 * p[0] + (trace - (sxy + sxz + syz))
    third = h36 * (1.0 / 3.0)
    mxx, myy, mzz = sx - third, sy - third, sz - third
    hcx = 2.0 * o[0] + ((o[3] + o[4]) + (o[5] + o[6]))
    hcy = 2.0 * o[1] + ((o[3] - o[4]) + (o[7] + o[8]))
    hcz = 2.0 * o[2] + ((o[5] - o[6]) + (o[7] - o[8]))
    nx = mxx * ux + dxy * uy + dxz * uz
    ny = dxy * ux + myy * uy + dyz * uz
    nz = dxz * ux + dyz * uy + mzz * uz
    q = ux * nx + uy * ny + uz * nz
    first = ux * hcx + uy * hcy + uz * hcz
    g4 = 0.4 * g
    b = g4 * g
    a = g * (1.0 / 12.0) + (1.0 / 60.0)
    gain = rho * (first * (1.0 / 12.0) + g4 * q)
    inlet = node == 1
    wall = node == 2
    vx = a * hcx + b * nx + jnp.where(inlet, 1.0, 0.0)
    vy = a * hcy + b * ny
    vz = a * hcz + b * nz
    base = h36 * (1.1 / 36.0) + trace * (1.0 / 120.0) - (0.5 * b) * q
    ex, ey, ez = -0.025 * mxx, -0.025 * myy, -0.025 * mzz
    bx, by = base + ex, base + ey
    bz = base + ez
    bxy, bxz, byz = bx + ey, bx + ez, by + ez
    wxy, wxz, wyz = 0.05 * dxy, 0.05 * dxz, 0.05 * dyz
    even = [bx, by, bz, bxy - wxy, bxy + wxy, bxz - wxz, bxz + wxz, byz - wyz, byz + wyz]
    odd = [vx, vy, vz, vx + vy, vx - vy, vx + vz, vx - vz, vy + vz, vy - vz]
    new = [jnp.where(wall, p[0], base - 0.4 * p[0])]
    for k in range(9):
        up = even[k] - 0.2 * e[k]
        down = odd[k] - 0.1 * o[k]
        new.append(jnp.where(wall, p[2 * k + 2], up + down))
        new.append(jnp.where(wall, p[2 * k + 1], up - down))
    return new, jnp.where(wall, 0.0, gain)


def lattice_kernel(
    adj_hbm,
    rho_hbm,
    vel_hbm,
    por_hbm,
    node_hbm,
    sens_hbm,
    field,
    sens,
    rho,
    vel,
    por,
    node,
    x_out,
    y_out,
    z_out,
    xy_out,
    xz_out,
    x_in,
    y_in,
    z_in,
    xy_in,
    yz_in,
    xz_in,
    load_sem,
    send_sem,
    recv_sem,
):
    here = [lax.axis_index(a) for a in AXES]
    size = [lax.axis_size(a) for a in AXES]

    def device(route):
        return tuple(lax.rem(h + (d + n), n) if d else h for h, d, n in zip(here, route, size))

    barrier = pltpu.get_barrier_semaphore()
    for route in ROUTES:
        pl.semaphore_signal(
            barrier, inc=1, device_id=device(route), device_id_type=pl.DeviceIdType.MESH
        )
    own = pl.ds(PZ, ROWS)
    loads = [
        pltpu.make_async_copy(src, dst, load_sem.at[k])
        for k, (src, dst) in enumerate(
            [
                (adj_hbm, field.at[0, :, own, :]),
                (rho_hbm, rho),
                (vel_hbm, vel),
                (por_hbm, por),
                (node_hbm, node),
                (sens_hbm, sens.at[0]),
            ]
        )
    ]
    for copy in loads:
        copy.start()

    lane = lax.broadcasted_iota(jnp.int32, (PZ, PY), 1)
    row = lax.broadcasted_iota(jnp.int32, (PZ, PY), 0)

    def plane(x):
        if isinstance(x, int):
            return pl.ds(x * PZ, PZ)
        return pl.ds(pl.multiple_of(x * PZ, PZ), PZ)

    def pack_columns(step, x, tiles):
        made = []
        for s in range(2):
            tile = tiles[s]
            for j, i in enumerate(CROSS_Y[s]):
                at = x + j * PX
                value = field[step, i, plane(x + 1), :]
                turned = pltpu.roll(value, at if s == 0 else at + 1, axis=1)
                tile = jnp.where(lane == at, turned, tile)
            made.append(tile)
        return tuple(made)

    def pull_y(step, i, x, tile, at):
        cy = VELOCITIES[i][1]
        edge = PY - 1 if cy == 1 else 0
        shift = (edge - at) % PY if isinstance(at, int) else (edge or PY) - at
        column = pltpu.roll(tile, shift, axis=1)
        value = pltpu.roll(field[step, i, plane(x + 1), :], PY - 1 if cy == 1 else 1, axis=1)
        field[step, i, plane(x + 1), :] = jnp.where(lane == edge, column, value)

    def transfer(step, route):
        dx, dy, dz = route
        if route in FACES_X:
            src, dst = x_out.at[step, side(dx)], x_in.at[step, side(dx)]
        elif route in FACES_Z:
            src, dst = z_out.at[step, side(dz)], z_in.at[step, side(dz)]
        elif route in FACES_Y:
            src, dst = y_out.at[step, side(dy)], y_in.at[step, side(dy)]
        elif route in EDGES_XY:
            src, dst = xy_out.at[step, side(dy)], xy_in.at[step, side(dx), side(dy)]
        elif route in EDGES_YZ:
            src, dst = y_out.at[step, side(dy)], yz_in.at[step, side(dy), side(dz)]
        else:
            src, dst = xz_out.at[step, side(dx)], xz_in.at[step, side(dx), side(dz)]
        k = ROUTES.index(route)
        return pltpu.make_async_remote_copy(
            src_ref=src,
            dst_ref=dst,
            send_sem=send_sem.at[step, k],
            recv_sem=recv_sem.at[step, k],
            device_id=device(route),
            device_id_type=pl.DeviceIdType.MESH,
        )

    def pack_far(step, tiles):
        for s in range(2):
            xy_out[step, s] = tiles[s]
            for j, i in enumerate(CROSS_X[s]):
                value = field[step, i, plane(PX if s else 1), :]
                x_out[step, s, j] = value
                cz = VELOCITIES[i][2]
                if cz:
                    at = side(-cz) * (PZ - 1)
                    xz_out[step, s, pl.ds(at, 1), :] = value[at : at + 1, :]

    def pack_near(step, tiles):
        for s in range(2):
            y_out[step, s] = tiles[s]
            for j, i in enumerate(CROSS_Z[s]):
                z_out[step, s, j] = field[step, i, pl.ds(PZ + s * (PZ - 1), PX, stride=PZ), :]

    def send(step, routes):
        for route in routes:
            transfer(step, route).start()

    def insert_y(step):
        for route in FACES_Y + EDGES_YZ:
            transfer(step, route).wait_recv()
        tiles = {}
        for s in range(2):
            for i in CROSS_Y[s]:
                cz = VELOCITIES[i][2]
                tiles[i] = y_in[step, s]
                if cz:
                    tiles[i] = jnp.where(
                        row == (0 if cz == 1 else PZ - 1), yz_in[step, s, side(-cz)], tiles[i]
                    )

        def body(x, carry):
            for s in range(2):
                for j, i in enumerate(CROSS_Y[s]):
                    pull_y(step, i, x, tiles[i], x + j * PX)
            return carry

        lax.fori_loop(0, PX, body, 0, unroll=4)

    def insert_z(step):
        for route in FACES_Z:
            transfer(step, route).wait_recv()
        wide = lax.broadcasted_iota(jnp.int32, (PX, PY), 1)
        for s in range(2):
            for j, i in enumerate(CROSS_Z[s]):
                rows = pl.ds(PZ + s * (PZ - 1), PX, stride=PZ)
                value = z_in[step, s, j]
                cy = VELOCITIES[i][1]
                if cy:
                    value = pltpu.roll(value, PY - 1 if cy == 1 else 1, axis=1)
                    value = jnp.where(
                        wide == (PY - 1 if cy == 1 else 0), field[step, i, rows, :], value
                    )
                field[step, i, rows, :] = value

    def insert_x(step):
        for route in FACES_X + EDGES_XY + EDGES_XZ:
            transfer(step, route).wait_recv()
        for s in range(2):
            for j, i in enumerate(CROSS_X[s]):
                field[step, i, plane(0 if s else PX + 1), :] = x_in[step, s, j]
        for dx, _, dz in EDGES_XZ:
            i = VELOCITIES.index((-dx, 0, -dz))
            at = (0 if dx == 1 else PZ * (PX + 1)) + side(dz) * (PZ - 1)
            field[step, i, pl.ds(at, 1), :] = xz_in[
                step, side(dx), side(dz), pl.ds(side(dz) * (PZ - 1), 1), :
            ]
        for dx, dy, _ in EDGES_XY:
            i = VELOCITIES.index((-dx, -dy, 0))
            at = CROSS_Y[side(dy)].index(i) * PX + (PX - 1 if dx == 1 else 0)
            pull_y(step, i, -1 if dx == 1 else PX, xy_in[step, side(dx), side(dy)], at)

    def advance(old, new, x):
        pulled = []
        for i, (cx, cy, cz) in enumerate(VELOCITIES):
            value = field[old, i, plane(x + (1 + cx)), :]
            if cz:
                value = pltpu.roll(value, PZ - 1 if cz == 1 else 1, axis=0)
            pulled.append(value)
        rows = plane(x)
        u = [vel[d, rows, :] for d in range(3)]
        made, gain = collide(pulled, rho[rows, :], u, por[rows, :], node[rows, :])
        for i in range(19):
            field[new, i, plane(x + 1), :] = made[i]
        sens[new, rows, :] = sens[old, rows, :] + gain

    def one_step(step, carry):
        def inner(x, c):
            advance(step, step + 1, x)
            return c

        insert_y(step)
        insert_z(step)
        insert_x(step)
        for x in (0, PX - 1):
            advance(step, step + 1, x)

        @pl.when(step == 0)
        def _():
            tiles = (blank,) * 2
            for x in (0, PX - 1):
                tiles = pack_columns(1, x, tiles)
            pack_far(1, tiles)
            send(1, FAR)

        lax.fori_loop(1, PX - 1, inner, 0, unroll=2)

        @pl.when(step == 0)
        def _():
            tiles = (xy_out[1, 0], xy_out[1, 1])
            for x in range(1, PX - 1):
                tiles = pack_columns(1, x, tiles)
            pack_near(1, tiles)
            send(1, NEAR)

        return carry

    blank = jnp.zeros((PZ, PY), jnp.float32)
    loads[0].wait()
    tiles = (blank,) * 2
    for x in range(PX):
        tiles = pack_columns(0, x, tiles)
    pack_far(0, tiles)
    pack_near(0, tiles)
    pl.semaphore_wait(barrier, len(ROUTES))
    send(0, FAR[:8])
    send(0, NEAR)
    send(0, FAR[8:])
    for copy in loads[1:]:
        copy.wait()
    lax.fori_loop(0, 2, one_step, 0)
    for step in range(2):
        for route in ROUTES:
            transfer(step, route).wait_send()


def store_kernel(field, sens, out_hbm, out_sens_hbm, sem):
    copies = [
        pltpu.make_async_copy(field.at[2, :, pl.ds(PZ, ROWS), :], out_hbm, sem.at[0]),
        pltpu.make_async_copy(sens.at[2], out_sens_hbm, sem.at[1]),
    ]
    for copy in copies:
        copy.start()
    for copy in copies:
        copy.wait()


def shards(adjoint, density, velocity, porosity, node_type, sensitivity_in):
    f32 = jnp.float32
    dma = pltpu.SemaphoreType.DMA
    anywhere = pl.BlockSpec(memory_space=pl.ANY)
    made = pl.pallas_call(
        lattice_kernel,
        out_shape=(
            pltpu.VMEM((3, 19, ROWS + 2 * PZ, PY), f32),
            pltpu.VMEM((3, ROWS, PY), f32),
        ),
        in_specs=[anywhere] * 6,
        out_specs=(pl.BlockSpec(memory_space=pltpu.VMEM),) * 2,
        scratch_shapes=[
            pltpu.VMEM((ROWS, PY), f32),
            pltpu.VMEM((3, ROWS, PY), f32),
            pltpu.VMEM((ROWS, PY), f32),
            pltpu.VMEM((ROWS, PY), jnp.int32),
            pltpu.VMEM((2, 2, 5, PZ, PY), f32),
            pltpu.VMEM((2, 2, PZ, PY), f32),
            pltpu.VMEM((2, 2, 5, PX, PY), f32),
            pltpu.VMEM((2, 2, PZ, PY), f32),
            pltpu.VMEM((2, 2, PZ, PY), f32),
            pltpu.VMEM((2, 2, 5, PZ, PY), f32),
            pltpu.VMEM((2, 2, PZ, PY), f32),
            pltpu.VMEM((2, 2, 5, PX, PY), f32),
            pltpu.VMEM((2, 2, 2, PZ, PY), f32),
            pltpu.VMEM((2, 2, 2, PZ, PY), f32),
            pltpu.VMEM((2, 2, 2, PZ, PY), f32),
            dma((6,)),
            dma((2, len(ROUTES))),
            dma((2, len(ROUTES))),
        ],
        compiler_params=pltpu.CompilerParams(
            collective_id=0, has_side_effects=True, vmem_limit_bytes=56 * 1024 * 1024
        ),
    )(
        adjoint.reshape(19, ROWS, PY),
        density.reshape(ROWS, PY),
        velocity.reshape(3, ROWS, PY),
        porosity.reshape(ROWS, PY),
        node_type.reshape(ROWS, PY),
        sensitivity_in.reshape(ROWS, PY),
    )
    out, sens = pl.pallas_call(
        store_kernel,
        out_shape=(
            jax.ShapeDtypeStruct((19, ROWS, PY), f32),
            jax.ShapeDtypeStruct((ROWS, PY), f32),
        ),
        in_specs=[anywhere] * 2,
        out_specs=(anywhere, anywhere),
        scratch_shapes=[dma((2,))],
        compiler_params=pltpu.CompilerParams(vmem_limit_bytes=1024 * 1024),
    )(*made)
    return out.reshape(19, PX, PZ, PY), sens.reshape(PX, PZ, PY)


def solution(mesh):
    cells = P("gx", "gz", "gy")
    many = P(None, "gx", "gz", "gy")
    return jax.shard_map(
        shards,
        mesh=mesh,
        in_specs=(many, cells, many, cells, cells, cells),
        out_specs=(many, cells),
        check_vma=False,
    )
```

```python
import functools

import jax
import jax.numpy as jnp
from jax import lax
from jax.experimental import pallas as pl
from jax.experimental.pallas import tpu as pltpu
from jax.sharding import PartitionSpec as P

AXES = ("gx", "gy", "gz")
PX, PZ, PY = 16, 8, 128
ROWS = PX * PZ

VELOCITIES = [
    (0, 0, 0),
    (1, 0, 0),
    (-1, 0, 0),
    (0, 1, 0),
    (0, -1, 0),
    (0, 0, 1),
    (0, 0, -1),
    (1, 1, 0),
    (-1, -1, 0),
    (1, -1, 0),
    (-1, 1, 0),
    (1, 0, 1),
    (-1, 0, -1),
    (1, 0, -1),
    (-1, 0, 1),
    (0, 1, 1),
    (0, -1, -1),
    (0, 1, -1),
    (0, -1, 1),
]
CROSS = [[[i for i, c in enumerate(VELOCITIES) if c[a] == s] for s in (1, -1)] for a in range(3)]
CROSS_X, CROSS_Y, CROSS_Z = CROSS
FACES_X = [(-1, 0, 0), (1, 0, 0)]
FACES_Y = [(0, -1, 0), (0, 1, 0)]
FACES_Z = [(0, 0, -1), (0, 0, 1)]
EDGES_XY = [(a, b, 0) for a in (-1, 1) for b in (-1, 1)]
EDGES_YZ = [(0, a, b) for a in (-1, 1) for b in (-1, 1)]
EDGES_XZ = [(a, 0, b) for a in (-1, 1) for b in (-1, 1)]
FAR = EDGES_XZ + EDGES_XY + FACES_X
NEAR = EDGES_YZ + FACES_Y
ROUTES = FAR + FACES_Z + NEAR
CORNERS = EDGES_XZ + EDGES_XY
GROUP_FAR, GROUP_Z, GROUP_NEAR = 0, 1, 3


def side(sign):
    return (sign + 1) // 2


def collide(p, rho, u, g, node):
    ux, uy, uz = u
    e = [p[i] + p[i + 1] for i in range(1, 19, 2)]
    o = [p[i] - p[i + 1] for i in range(1, 19, 2)]
    sxy, sxz, syz = e[3] + e[4], e[5] + e[6], e[7] + e[8]
    dxy, dxz, dyz = e[3] - e[4], e[5] - e[6], e[7] - e[8]
    sx = 2.0 * e[0] + (sxy + sxz)
    sy = 2.0 * e[1] + (sxy + syz)
    sz = 2.0 * e[2] + (sxz + syz)
    trace = sx + sy + sz
    h36 = 12.0 * p[0] + (trace - (sxy + sxz + syz))
    third = h36 * (1.0 / 3.0)
    mxx, myy, mzz = sx - third, sy - third, sz - third
    hcx = 2.0 * o[0] + ((o[3] + o[4]) + (o[5] + o[6]))
    hcy = 2.0 * o[1] + ((o[3] - o[4]) + (o[7] + o[8]))
    hcz = 2.0 * o[2] + ((o[5] - o[6]) + (o[7] - o[8]))
    nx = mxx * ux + dxy * uy + dxz * uz
    ny = dxy * ux + myy * uy + dyz * uz
    nz = dxz * ux + dyz * uy + mzz * uz
    q = ux * nx + uy * ny + uz * nz
    first = ux * hcx + uy * hcy + uz * hcz
    g4 = 0.4 * g
    b = g4 * g
    a = g * (1.0 / 12.0) + (1.0 / 60.0)
    gain = rho * (first * (1.0 / 12.0) + g4 * q)
    inlet = node == 1
    wall = node == 2
    vx = a * hcx + b * nx + jnp.where(inlet, 1.0, 0.0)
    vy = a * hcy + b * ny
    vz = a * hcz + b * nz
    base = h36 * (1.1 / 36.0) + trace * (1.0 / 120.0) - (0.5 * b) * q
    ex, ey, ez = -0.025 * mxx, -0.025 * myy, -0.025 * mzz
    bx, by = base + ex, base + ey
    bz = base + ez
    bxy, bxz, byz = bx + ey, bx + ez, by + ez
    wxy, wxz, wyz = 0.05 * dxy, 0.05 * dxz, 0.05 * dyz
    even = [bx, by, bz, bxy - wxy, bxy + wxy, bxz - wxz, bxz + wxz, byz - wyz, byz + wyz]
    odd = [vx, vy, vz, vx + vy, vx - vy, vx + vz, vx - vz, vy + vz, vy - vz]
    new = [jnp.where(wall, p[0], base - 0.4 * p[0])]
    for k in range(9):
        up = even[k] - 0.2 * e[k]
        down = odd[k] - 0.1 * o[k]
        new.append(jnp.where(wall, p[2 * k + 2], up + down))
        new.append(jnp.where(wall, p[2 * k + 1], up - down))
    return new, jnp.where(wall, 0.0, gain)


def plane(x):
    if isinstance(x, int):
        return pl.ds(x * PZ, PZ)
    return pl.ds(pl.multiple_of(x * PZ, PZ), PZ)


def advance(old, rows, rho, vel, por, node):
    pulled = []
    for value, (_, _, cz) in zip(old, VELOCITIES):
        if cz:
            value = pltpu.roll(value, PZ - 1 if cz == 1 else 1, axis=0)
        pulled.append(value)
    u = [vel[d, rows, :] for d in range(3)]
    return collide(pulled, rho[rows, :], u, por[rows, :], node[rows, :])


def lattice_kernel(
    adj_hbm,
    rho_hbm,
    vel_hbm,
    por_hbm,
    node_hbm,
    sens_hbm,
    field,
    sens,
    rho,
    vel,
    por,
    node,
    x_out,
    y_out,
    z_out,
    xy_out,
    xz_out,
    far_in,
    near_in,
    z_in,
    load_sem,
    send_sem,
    recv_sem,
):
    here = [lax.axis_index(a) for a in AXES]
    size = [lax.axis_size(a) for a in AXES]

    def device(route):
        return tuple(lax.rem(h + (d + n), n) if d else h for h, d, n in zip(here, route, size))

    barrier = pltpu.get_barrier_semaphore()
    for route in ROUTES:
        pl.semaphore_signal(
            barrier, inc=1, device_id=device(route), device_id_type=pl.DeviceIdType.MESH
        )
    own = pl.ds(PZ, ROWS)
    loads = [
        pltpu.make_async_copy(src, dst, load_sem.at[k])
        for k, (src, dst) in enumerate(
            [
                (adj_hbm, field.at[0, :, own, :]),
                (rho_hbm, rho),
                (vel_hbm, vel),
                (por_hbm, por),
                (node_hbm, node),
                (sens_hbm, sens.at[0]),
            ]
        )
    ]
    for copy in loads:
        copy.start()

    lane = lax.broadcasted_iota(jnp.int32, (PZ, PY), 1)
    row = lax.broadcasted_iota(jnp.int32, (PZ, PY), 0)

    def pack_columns(step, x, tiles):
        made = []
        for s in range(2):
            tile = tiles[s]
            for j, i in enumerate(CROSS_Y[s]):
                at = x + j * PX
                value = field[step, i, plane(x + 1), :]
                turned = pltpu.roll(value, at if s == 0 else at + 1, axis=1)
                tile = jnp.where(lane == at, turned, tile)
            made.append(tile)
        return tuple(made)

    def pull_y(step, i, x, tile, at):
        cy = VELOCITIES[i][1]
        edge = PY - 1 if cy == 1 else 0
        shift = (edge - at) % PY if isinstance(at, int) else (edge or PY) - at
        column = pltpu.roll(tile, shift, axis=1)
        value = pltpu.roll(field[step, i, plane(x + 1), :], PY - 1 if cy == 1 else 1, axis=1)
        field[step, i, plane(x + 1), :] = jnp.where(lane == edge, column, value)

    def x_part(buffer, step, s):
        return buffer.at[step, pl.ds(len(CORNERS) + 5 * s, 5)]

    def copy_of(step, group, src, dst, route):
        return pltpu.make_async_remote_copy(
            src_ref=src,
            dst_ref=dst,
            send_sem=send_sem.at[step, group],
            recv_sem=recv_sem.at[step, group],
            device_id=device(route),
            device_id_type=pl.DeviceIdType.MESH,
        )

    def transfer(step, route, half=0):
        dx, dy, dz = route
        if route in FACES_X:
            src, dst = x_out.at[step, side(dx)], x_part(far_in, step, side(dx))
        elif route in FACES_Z:
            src, dst = z_out.at[step, half, side(dz)], z_in.at[step, half, side(dz)]
        elif route in NEAR:
            src, dst = y_out.at[step, side(dy)], near_in.at[step, NEAR.index(route)]
        elif route in EDGES_XY:
            src, dst = xy_out.at[step, side(dy)], far_in.at[step, CORNERS.index(route)]
        else:
            src, dst = xz_out.at[step, side(dx)], far_in.at[step, CORNERS.index(route)]
        if route in FACES_Z:
            return copy_of(step, GROUP_Z + half, src, dst, route)
        return copy_of(step, GROUP_NEAR if route in NEAR else GROUP_FAR, src, dst, route)

    def whole(step, group):
        if group == GROUP_FAR:
            buffer = far_in.at[step]
        elif group == GROUP_NEAR:
            buffer = near_in.at[step]
        else:
            buffer = z_in.at[step, group - GROUP_Z]
        return copy_of(step, group, buffer, buffer, FACES_X[0])

    def pack_xz(step):
        for s in range(2):
            for i in CROSS_X[s]:
                cz = VELOCITIES[i][2]
                if cz:
                    at = side(-cz) * (PZ - 1)
                    line = pl.ds(PZ * (PX if s else 1) + at, 1)
                    xz_out[step, s, pl.ds(at, 1), :] = field[step, i, line, :]

    def pack_x(step, tiles):
        for s in range(2):
            xy_out[step, s] = tiles[s]
            for j, i in enumerate(CROSS_X[s]):
                x_out[step, s, j] = field[step, i, plane(PX if s else 1), :]

    def z_rows(s, half):
        return pl.ds(PZ + s * (PZ - 1) + half * (ROWS // 2), PX // 2, stride=PZ)

    def pack_z(step, half):
        for s in range(2):
            for j, i in enumerate(CROSS_Z[s]):
                z_out[step, half, s, j] = field[step, i, z_rows(s, half), :]

    def send_z(step, half):
        for route in FACES_Z:
            transfer(step, route, half).start()

    def pack_near(step, tiles):
        for s in range(2):
            y_out[step, s] = tiles[s]

    def send(step, routes):
        for route in routes:
            transfer(step, route).start()

    def insert_y(step):
        whole(step, GROUP_NEAR).wait_recv()
        tiles = {}
        for s in range(2):
            for i in CROSS_Y[s]:
                cz = VELOCITIES[i][2]
                tiles[i] = near_in[step, NEAR.index(FACES_Y[s])]
                if cz:
                    corner = near_in[step, NEAR.index((0, 2 * s - 1, -cz))]
                    tiles[i] = jnp.where(row == (0 if cz == 1 else PZ - 1), corner, tiles[i])

        def body(x, carry):
            for s in range(2):
                for j, i in enumerate(CROSS_Y[s]):
                    pull_y(step, i, x, tiles[i], x + j * PX)
            return carry

        lax.fori_loop(0, PX, body, 0, unroll=4)

    def insert_z(step, half):
        whole(step, GROUP_Z + half).wait_recv()
        for s in range(2):
            for j, i in enumerate(CROSS_Z[s]):
                rows = z_rows(s, half)
                value = z_in[step, half, s, j]
                cy = VELOCITIES[i][1]
                if cy:
                    value = pltpu.roll(value, PY - 1 if cy == 1 else 1, axis=1)
                    value = jnp.where(
                        lane == (PY - 1 if cy == 1 else 0), field[step, i, rows, :], value
                    )
                field[step, i, rows, :] = value

    def insert_x(step):
        whole(step, GROUP_FAR).wait_recv()
        for s in range(2):
            for j, i in enumerate(CROSS_X[s]):
                field[step, i, plane(0 if s else PX + 1), :] = far_in[
                    step, len(CORNERS) + 5 * s + j
                ]
        for route in EDGES_XZ:
            dx, _, dz = route
            i = VELOCITIES.index((-dx, 0, -dz))
            at = side(dz) * (PZ - 1)
            field[step, i, pl.ds((0 if dx == 1 else PZ * (PX + 1)) + at, 1), :] = far_in[
                step, CORNERS.index(route), pl.ds(at, 1), :
            ]
        for route in EDGES_XY:
            dx, dy, _ = route
            i = VELOCITIES.index((-dx, -dy, 0))
            at = CROSS_Y[side(dy)].index(i) * PX + (PX - 1 if dx == 1 else 0)
            tile = far_in[step, CORNERS.index(route)]
            pull_y(step, i, -1 if dx == 1 else PX, tile, at)

    def step_plane(step, x):
        old = [field[step, i, plane(x + 1 + c[0]), :] for i, c in enumerate(VELOCITIES)]
        rows = plane(x)
        new, gain = advance(old, rows, rho, vel, por, node)
        for i in range(19):
            field[step + 1, i, plane(x + 1), :] = new[i]
        sens[step + 1, rows, :] = sens[step, rows, :] + gain

    def one_step(step, carry):
        def pair(k, c):
            step_plane(step, 2 * k + 1)
            step_plane(step, 2 * k + 2)
            return c

        def part(half, c):
            @pl.when(jnp.logical_and(step == 1, half == 1))
            def _():
                insert_z(1, 1)

            lax.fori_loop(3 * half, 3 + 4 * half, pair, 0)

            @pl.when(jnp.logical_and(step == 0, half == 0))
            def _():
                pack_z(1, 0)
                send_z(1, 0)

            return c

        insert_y(step)
        insert_z(step, 0)

        @pl.when(step == 0)
        def _():
            insert_z(0, 1)
            insert_x(0)
            for x in (0, PX - 1):
                step_plane(0, x)
            pack_xz(1)
            send(1, EDGES_XZ)
            step_plane(0, PX // 2 - 1)
            tiles = (blank,) * 2
            for x in (0, PX - 1):
                tiles = pack_columns(1, x, tiles)
            pack_x(1, tiles)
            send(1, EDGES_XY + FACES_X)

        lax.fori_loop(0, 2, part, 0)

        @pl.when(step == 0)
        def _():
            pack_z(1, 1)
            send_z(1, 1)
            tiles = (xy_out[1, 0], xy_out[1, 1])
            for x in range(1, PX - 1):
                tiles = pack_columns(1, x, tiles)
            pack_near(1, tiles)
            send(1, NEAR)
            for group in range(4):
                whole(0, group).wait_send()

        return carry

    blank = jnp.zeros((PZ, PY), jnp.float32)
    loads[0].wait()
    tiles = (blank,) * 2
    for x in range(PX):
        tiles = pack_columns(0, x, tiles)
    pack_xz(0)
    pack_x(0, tiles)
    pack_near(0, tiles)
    pack_z(0, 0)
    pack_z(0, 1)
    pl.semaphore_wait(barrier, len(ROUTES))
    send(0, EDGES_XZ)
    send_z(0, 0)
    send_z(0, 1)
    send(0, EDGES_XY + FACES_X + NEAR)
    for copy in loads[1:]:
        copy.wait()
    lax.fori_loop(0, 2, one_step, 0)
    insert_x(1)
    for group in range(4):
        whole(1, group).wait_send()


def last_kernel(field, sens, rho, vel, por, node, out_hbm, out_sens_hbm, result, gained, sem):
    inner = pl.ds(PZ, ROWS - 2 * PZ)
    copies = [
        pltpu.make_async_copy(
            field.at[2, :, pl.ds(2 * PZ, ROWS - 2 * PZ), :], out_hbm.at[:, inner, :], sem.at[0]
        ),
        pltpu.make_async_copy(sens.at[2, inner, :], out_sens_hbm.at[inner, :], sem.at[1]),
    ]
    for copy in copies:
        copy.start()
    for k, x in enumerate((0, PX - 1)):
        old = [field[1, i, plane(x + 1 + c[0]), :] for i, c in enumerate(VELOCITIES)]
        rows = plane(x)
        new, gain = advance(old, rows, rho, vel, por, node)
        for i in range(19):
            result[k, i] = new[i]
        gained[k] = sens[1, rows, :] + gain
    for k, x in enumerate((0, PX - 1)):
        rows = plane(x)
        copies.append(
            pltpu.make_async_copy(result.at[k], out_hbm.at[:, rows, :], sem.at[2 + 2 * k])
        )
        copies.append(
            pltpu.make_async_copy(gained.at[k], out_sens_hbm.at[rows, :], sem.at[3 + 2 * k])
        )
    for copy in copies[2:]:
        copy.start()
    for copy in copies:
        copy.wait()


def shards(adjoint, density, velocity, porosity, node_type, sensitivity_in):
    f32 = jnp.float32
    dma = pltpu.SemaphoreType.DMA
    anywhere = pl.BlockSpec(memory_space=pl.ANY)
    vmem = pl.BlockSpec(memory_space=pltpu.VMEM)
    made = pl.pallas_call(
        lattice_kernel,
        out_shape=(
            pltpu.VMEM((3, 19, ROWS + 2 * PZ, PY), f32),
            pltpu.VMEM((3, ROWS, PY), f32),
            pltpu.VMEM((ROWS, PY), f32),
            pltpu.VMEM((3, ROWS, PY), f32),
            pltpu.VMEM((ROWS, PY), f32),
            pltpu.VMEM((ROWS, PY), jnp.int32),
        ),
        in_specs=[anywhere] * 6,
        out_specs=(vmem,) * 6,
        scratch_shapes=[
            pltpu.VMEM((2, 2, 5, PZ, PY), f32),
            pltpu.VMEM((2, 2, PZ, PY), f32),
            pltpu.VMEM((2, 2, 2, 5, PX // 2, PY), f32),
            pltpu.VMEM((2, 2, PZ, PY), f32),
            pltpu.VMEM((2, 2, PZ, PY), f32),
            pltpu.VMEM((2, len(CORNERS) + 10, PZ, PY), f32),
            pltpu.VMEM((2, len(NEAR), PZ, PY), f32),
            pltpu.VMEM((2, 2, 2, 5, PX // 2, PY), f32),
            dma((6,)),
            dma((2, 4)),
            dma((2, 4)),
        ],
        compiler_params=pltpu.CompilerParams(
            collective_id=0, has_side_effects=True, vmem_limit_bytes=56 * 1024 * 1024
        ),
    )(
        adjoint.reshape(19, ROWS, PY),
        density.reshape(ROWS, PY),
        velocity.reshape(3, ROWS, PY),
        porosity.reshape(ROWS, PY),
        node_type.reshape(ROWS, PY),
        sensitivity_in.reshape(ROWS, PY),
    )
    out, sens = pl.pallas_call(
        last_kernel,
        out_shape=(
            jax.ShapeDtypeStruct((19, ROWS, PY), f32),
            jax.ShapeDtypeStruct((ROWS, PY), f32),
        ),
        in_specs=[vmem] * 6,
        out_specs=(anywhere, anywhere),
        scratch_shapes=[
            pltpu.VMEM((2, 19, PZ, PY), f32),
            pltpu.VMEM((2, PZ, PY), f32),
            dma((6,)),
        ],
        compiler_params=pltpu.CompilerParams(vmem_limit_bytes=8 * 1024 * 1024),
    )(*made)
    return out.reshape(19, PX, PZ, PY), sens.reshape(PX, PZ, PY)


def solution(mesh):
    cells = P("gx", "gz", "gy")
    many = P(None, "gx", "gz", "gy")
    return jax.shard_map(
        shards,
        mesh=mesh,
        in_specs=(many, cells, many, cells, cells, cells),
        out_specs=(many, cells),
        check_vma=False,
    )
```

```python
import functools

import jax
import jax.numpy as jnp
from jax import lax
from jax.experimental import pallas as pl
from jax.experimental.pallas import tpu as pltpu
from jax.sharding import PartitionSpec as P

AXES = ("gx", "gy", "gz")
PX, PZ, PY = 16, 8, 128
ROWS = PX * PZ

VELOCITIES = [
    (0, 0, 0),
    (1, 0, 0),
    (-1, 0, 0),
    (0, 1, 0),
    (0, -1, 0),
    (0, 0, 1),
    (0, 0, -1),
    (1, 1, 0),
    (-1, -1, 0),
    (1, -1, 0),
    (-1, 1, 0),
    (1, 0, 1),
    (-1, 0, -1),
    (1, 0, -1),
    (-1, 0, 1),
    (0, 1, 1),
    (0, -1, -1),
    (0, 1, -1),
    (0, -1, 1),
]
CROSS = [[[i for i, c in enumerate(VELOCITIES) if c[a] == s] for s in (1, -1)] for a in range(3)]
CROSS_X, CROSS_Y, CROSS_Z = CROSS
FACES_X = [(-1, 0, 0), (1, 0, 0)]
FACES_Y = [(0, -1, 0), (0, 1, 0)]
FACES_Z = [(0, 0, -1), (0, 0, 1)]
EDGES_XY = [(a, b, 0) for a in (-1, 1) for b in (-1, 1)]
EDGES_YZ = [(0, a, b) for a in (-1, 1) for b in (-1, 1)]
EDGES_XZ = [(a, 0, b) for a in (-1, 1) for b in (-1, 1)]
FAR = EDGES_XZ + EDGES_XY + FACES_X
NEAR = EDGES_YZ + FACES_Y
ROUTES = FAR + FACES_Z + NEAR
CORNERS = EDGES_XZ + EDGES_XY
GROUP_FAR, GROUP_Z, GROUP_NEAR, GROUP_RELAY = 0, 1, 3, 4
GREETED = FACES_X + FACES_Z + NEAR


def side(sign):
    return (sign + 1) // 2


def collide(p, rho, u, g, node):
    ux, uy, uz = u
    e = [p[i] + p[i + 1] for i in range(1, 19, 2)]
    o = [p[i] - p[i + 1] for i in range(1, 19, 2)]
    sxy, sxz, syz = e[3] + e[4], e[5] + e[6], e[7] + e[8]
    dxy, dxz, dyz = e[3] - e[4], e[5] - e[6], e[7] - e[8]
    sx = 2.0 * e[0] + (sxy + sxz)
    sy = 2.0 * e[1] + (sxy + syz)
    sz = 2.0 * e[2] + (sxz + syz)
    trace = sx + sy + sz
    h36 = 12.0 * p[0] + (trace - (sxy + sxz + syz))
    third = h36 * (1.0 / 3.0)
    mxx, myy, mzz = sx - third, sy - third, sz - third
    hcx = 2.0 * o[0] + ((o[3] + o[4]) + (o[5] + o[6]))
    hcy = 2.0 * o[1] + ((o[3] - o[4]) + (o[7] + o[8]))
    hcz = 2.0 * o[2] + ((o[5] - o[6]) + (o[7] - o[8]))
    nx = mxx * ux + dxy * uy + dxz * uz
    ny = dxy * ux + myy * uy + dyz * uz
    nz = dxz * ux + dyz * uy + mzz * uz
    q = ux * nx + uy * ny + uz * nz
    first = ux * hcx + uy * hcy + uz * hcz
    g4 = 0.4 * g
    b = g4 * g
    a = g * (1.0 / 12.0) + (1.0 / 60.0)
    gain = rho * (first * (1.0 / 12.0) + g4 * q)
    inlet = node == 1
    wall = node == 2
    vx = a * hcx + b * nx + jnp.where(inlet, 1.0, 0.0)
    vy = a * hcy + b * ny
    vz = a * hcz + b * nz
    base = h36 * (1.1 / 36.0) + trace * (1.0 / 120.0) - (0.5 * b) * q
    ex, ey, ez = -0.025 * mxx, -0.025 * myy, -0.025 * mzz
    bx, by = base + ex, base + ey
    bz = base + ez
    bxy, bxz, byz = bx + ey, bx + ez, by + ez
    wxy, wxz, wyz = 0.05 * dxy, 0.05 * dxz, 0.05 * dyz
    even = [bx, by, bz, bxy - wxy, bxy + wxy, bxz - wxz, bxz + wxz, byz - wyz, byz + wyz]
    odd = [vx, vy, vz, vx + vy, vx - vy, vx + vz, vx - vz, vy + vz, vy - vz]
    new = [jnp.where(wall, p[0], base - 0.4 * p[0])]
    for k in range(9):
        up = even[k] - 0.2 * e[k]
        down = odd[k] - 0.1 * o[k]
        new.append(jnp.where(wall, p[2 * k + 2], up + down))
        new.append(jnp.where(wall, p[2 * k + 1], up - down))
    return new, jnp.where(wall, 0.0, gain)


def plane(x):
    if isinstance(x, int):
        return pl.ds(x * PZ, PZ)
    return pl.ds(pl.multiple_of(x * PZ, PZ), PZ)


def advance(old, rows, rho, vel, por, node):
    pulled = []
    for value, (_, _, cz) in zip(old, VELOCITIES):
        if cz:
            value = pltpu.roll(value, PZ - 1 if cz == 1 else 1, axis=0)
        pulled.append(value)
    u = [vel[d, rows, :] for d in range(3)]
    return collide(pulled, rho[rows, :], u, por[rows, :], node[rows, :])


def lattice_kernel(
    adj_hbm,
    rho_hbm,
    vel_hbm,
    por_hbm,
    node_hbm,
    sens_hbm,
    field,
    sens,
    rho,
    vel,
    por,
    node,
    x_out,
    y_out,
    z_out,
    xy_out,
    xz_out,
    far_in,
    near_in,
    z_in,
    relay_in,
    load_sem,
    send_sem,
    recv_sem,
):
    here = [lax.axis_index(a) for a in AXES]
    size = [lax.axis_size(a) for a in AXES]

    def device(route):
        return tuple(lax.rem(h + (d + n), n) if d else h for h, d, n in zip(here, route, size))

    barrier = pltpu.get_barrier_semaphore()
    for route in GREETED:
        pl.semaphore_signal(
            barrier, inc=1, device_id=device(route), device_id_type=pl.DeviceIdType.MESH
        )
    own = pl.ds(PZ, ROWS)
    loads = [
        pltpu.make_async_copy(src, dst, load_sem.at[k])
        for k, (src, dst) in enumerate(
            [
                (adj_hbm, field.at[0, :, own, :]),
                (rho_hbm, rho),
                (vel_hbm, vel),
                (por_hbm, por),
                (node_hbm, node),
                (sens_hbm, sens.at[0]),
            ]
        )
    ]
    for copy in loads:
        copy.start()

    lane = lax.broadcasted_iota(jnp.int32, (PZ, PY), 1)
    row = lax.broadcasted_iota(jnp.int32, (PZ, PY), 0)

    def pack_columns(step, x, tiles):
        made = []
        for s in range(2):
            tile = tiles[s]
            for j, i in enumerate(CROSS_Y[s]):
                at = x + j * PX
                value = field[step, i, plane(x + 1), :]
                turned = pltpu.roll(value, at if s == 0 else at + 1, axis=1)
                tile = jnp.where(lane == at, turned, tile)
            made.append(tile)
        return tuple(made)

    def pull_y(step, i, x, tile, at):
        cy = VELOCITIES[i][1]
        edge = PY - 1 if cy == 1 else 0
        shift = (edge - at) % PY if isinstance(at, int) else (edge or PY) - at
        column = pltpu.roll(tile, shift, axis=1)
        value = pltpu.roll(field[step, i, plane(x + 1), :], PY - 1 if cy == 1 else 1, axis=1)
        field[step, i, plane(x + 1), :] = jnp.where(lane == edge, column, value)

    def x_part(buffer, step, s):
        return buffer.at[step, pl.ds(len(CORNERS) + 5 * s, 5)]

    def copy_of(step, group, src, dst, route):
        return pltpu.make_async_remote_copy(
            src_ref=src,
            dst_ref=dst,
            send_sem=send_sem.at[step, group],
            recv_sem=recv_sem.at[step, group],
            device_id=device(route),
            device_id_type=pl.DeviceIdType.MESH,
        )

    def transfer(step, route, half=0):
        dx, dy, dz = route
        if route in FACES_X:
            src, dst = x_out.at[step, side(dx)], x_part(far_in, step, side(dx))
        elif route in FACES_Z:
            src, dst = z_out.at[step, half, side(dz)], z_in.at[step, half, side(dz)]
        elif route in NEAR:
            src, dst = y_out.at[step, side(dy)], near_in.at[step, NEAR.index(route)]
        elif route in EDGES_XY:
            src, dst = xy_out.at[step, side(dy)], far_in.at[step, CORNERS.index(route)]
        else:
            src, dst = xz_out.at[step, side(dz)], far_in.at[step, CORNERS.index(route)]
        if route in FACES_Z:
            return copy_of(step, GROUP_Z + half, src, dst, route)
        return copy_of(step, GROUP_NEAR if route in NEAR else GROUP_FAR, src, dst, route)

    def whole(step, group):
        if group == GROUP_FAR:
            buffer = far_in.at[step]
        elif group == GROUP_NEAR:
            buffer = near_in.at[step]
        elif group == GROUP_RELAY:
            buffer = relay_in
        else:
            buffer = z_in.at[step, group - GROUP_Z]
        return copy_of(step, group, buffer, buffer, FACES_X[0])

    def pack_xz(step):
        for s in range(2):
            for i in CROSS_Z[s]:
                cx = VELOCITIES[i][0]
                if cx:
                    line = pl.ds(PZ * (1 if cx == 1 else PX) + s * (PZ - 1), 1)
                    xz_out[step, s, pl.ds(side(-cx) * (PZ - 1), 1), :] = field[step, i, line, :]

    def send_corner_rows():
        for s, route in enumerate(FACES_Z):
            copy_of(0, GROUP_RELAY, xz_out.at[0, s], relay_in.at[s], route).start()

    def relay():
        def forward(src, dx, dy, dz):
            dst = far_in.at[0, CORNERS.index((dx, dy, dz))]
            copy_of(0, GROUP_FAR, src, dst, (dx, 0, 0)).start()

        whole(0, GROUP_RELAY).wait_recv()
        for dx in (-1, 1):
            for dz in (-1, 1):
                forward(relay_in.at[side(dz)], dx, 0, dz)
        whole(0, GROUP_NEAR).wait_recv()
        for dx in (-1, 1):
            for dy in (-1, 1):
                forward(near_in.at[0, NEAR.index((0, dy, 0))], dx, dy, 0)

    def pack_x(step, tiles):
        for s in range(2):
            xy_out[step, s] = tiles[s]
            for j, i in enumerate(CROSS_X[s]):
                x_out[step, s, j] = field[step, i, plane(PX if s else 1), :]

    def z_rows(s, half):
        return pl.ds(PZ + s * (PZ - 1) + half * (ROWS // 2), PX // 2, stride=PZ)

    def pack_z(step, half):
        for s in range(2):
            for j, i in enumerate(CROSS_Z[s]):
                z_out[step, half, s, j] = field[step, i, z_rows(s, half), :]

    def send_z(step, half):
        for route in FACES_Z:
            transfer(step, route, half).start()

    def pack_near(step, tiles):
        for s in range(2):
            y_out[step, s] = tiles[s]

    def send(step, routes):
        for route in routes:
            transfer(step, route).start()

    def insert_y(step):
        @pl.when(step == 1)
        def _():
            whole(1, GROUP_NEAR).wait_recv()

        tiles = {}
        for s in range(2):
            for i in CROSS_Y[s]:
                cz = VELOCITIES[i][2]
                tiles[i] = near_in[step, NEAR.index(FACES_Y[s])]
                if cz:
                    corner = near_in[step, NEAR.index((0, 2 * s - 1, -cz))]
                    tiles[i] = jnp.where(row == (0 if cz == 1 else PZ - 1), corner, tiles[i])

        def body(x, carry):
            for s in range(2):
                for j, i in enumerate(CROSS_Y[s]):
                    pull_y(step, i, x, tiles[i], x + j * PX)
            return carry

        lax.fori_loop(0, PX, body, 0, unroll=4)

    def insert_z(step, half):
        whole(step, GROUP_Z + half).wait_recv()
        for s in range(2):
            for j, i in enumerate(CROSS_Z[s]):
                rows = z_rows(s, half)
                value = z_in[step, half, s, j]
                cy = VELOCITIES[i][1]
                if cy:
                    value = pltpu.roll(value, PY - 1 if cy == 1 else 1, axis=1)
                    value = jnp.where(
                        lane == (PY - 1 if cy == 1 else 0), field[step, i, rows, :], value
                    )
                field[step, i, rows, :] = value

    def insert_x(step):
        whole(step, GROUP_FAR).wait_recv()
        for s in range(2):
            for j, i in enumerate(CROSS_X[s]):
                field[step, i, plane(0 if s else PX + 1), :] = far_in[
                    step, len(CORNERS) + 5 * s + j
                ]
        for route in EDGES_XZ:
            dx, _, dz = route
            i = VELOCITIES.index((-dx, 0, -dz))
            at = side(dz) * (PZ - 1)
            field[step, i, pl.ds((0 if dx == 1 else PZ * (PX + 1)) + at, 1), :] = far_in[
                step, CORNERS.index(route), pl.ds(side(dx) * (PZ - 1), 1), :
            ]
        for route in EDGES_XY:
            dx, dy, _ = route
            i = VELOCITIES.index((-dx, -dy, 0))
            at = CROSS_Y[side(dy)].index(i) * PX + (PX - 1 if dx == 1 else 0)
            tile = far_in[step, CORNERS.index(route)]
            pull_y(step, i, -1 if dx == 1 else PX, tile, at)

    def step_plane(step, x):
        old = [field[step, i, plane(x + 1 + c[0]), :] for i, c in enumerate(VELOCITIES)]
        rows = plane(x)
        new, gain = advance(old, rows, rho, vel, por, node)
        for i in range(19):
            field[step + 1, i, plane(x + 1), :] = new[i]
        sens[step + 1, rows, :] = sens[step, rows, :] + gain

    def one_step(step, carry):
        def pair(k, c):
            step_plane(step, 2 * k + 1)
            step_plane(step, 2 * k + 2)
            return c

        def part(half, c):
            @pl.when(jnp.logical_and(step == 1, half == 1))
            def _():
                insert_z(1, 1)

            lax.fori_loop(3 * half, 3 + 4 * half, pair, 0)

            @pl.when(jnp.logical_and(step == 0, half == 0))
            def _():
                pack_z(1, 0)
                send_z(1, 0)

            return c

        insert_y(step)
        insert_z(step, 0)

        @pl.when(step == 0)
        def _():
            insert_z(0, 1)
            insert_x(0)
            for x in (0, PX - 1):
                step_plane(0, x)
            pack_xz(1)
            send(1, EDGES_XZ)
            step_plane(0, PX // 2 - 1)
            tiles = (blank,) * 2
            for x in (0, PX - 1):
                tiles = pack_columns(1, x, tiles)
            pack_x(1, tiles)
            send(1, EDGES_XY + FACES_X)

        lax.fori_loop(0, 2, part, 0)

        @pl.when(step == 0)
        def _():
            pack_z(1, 1)
            send_z(1, 1)
            tiles = (xy_out[1, 0], xy_out[1, 1])
            for x in range(1, PX - 1):
                tiles = pack_columns(1, x, tiles)
            pack_near(1, tiles)
            send(1, NEAR)
            for group in range(5):
                whole(0, group).wait_send()

        return carry

    blank = jnp.zeros((PZ, PY), jnp.float32)
    loads[0].wait()
    tiles = (blank,) * 2
    for x in range(PX):
        tiles = pack_columns(0, x, tiles)
    pack_xz(0)
    pack_x(0, tiles)
    pack_near(0, tiles)
    pack_z(0, 0)
    pack_z(0, 1)
    pl.semaphore_wait(barrier, len(GREETED))
    send_corner_rows()
    send(0, NEAR)
    send_z(0, 0)
    send_z(0, 1)
    send(0, FACES_X)
    for copy in loads[1:]:
        copy.wait()
    relay()
    lax.fori_loop(0, 2, one_step, 0)
    insert_x(1)
    for group in range(4):
        whole(1, group).wait_send()


def last_kernel(field, sens, rho, vel, por, node, out_hbm, out_sens_hbm, result, gained, sem):
    inner = pl.ds(PZ, ROWS - 2 * PZ)
    copies = [
        pltpu.make_async_copy(
            field.at[2, :, pl.ds(2 * PZ, ROWS - 2 * PZ), :], out_hbm.at[:, inner, :], sem.at[0]
        ),
        pltpu.make_async_copy(sens.at[2, inner, :], out_sens_hbm.at[inner, :], sem.at[1]),
    ]
    for copy in copies:
        copy.start()
    for k, x in enumerate((0, PX - 1)):
        old = [field[1, i, plane(x + 1 + c[0]), :] for i, c in enumerate(VELOCITIES)]
        rows = plane(x)
        new, gain = advance(old, rows, rho, vel, por, node)
        for i in range(19):
            result[k, i] = new[i]
        gained[k] = sens[1, rows, :] + gain
    for k, x in enumerate((0, PX - 1)):
        rows = plane(x)
        copies.append(
            pltpu.make_async_copy(result.at[k], out_hbm.at[:, rows, :], sem.at[2 + 2 * k])
        )
        copies.append(
            pltpu.make_async_copy(gained.at[k], out_sens_hbm.at[rows, :], sem.at[3 + 2 * k])
        )
    for copy in copies[2:]:
        copy.start()
    for copy in copies:
        copy.wait()


def shards(adjoint, density, velocity, porosity, node_type, sensitivity_in):
    f32 = jnp.float32
    dma = pltpu.SemaphoreType.DMA
    anywhere = pl.BlockSpec(memory_space=pl.ANY)
    vmem = pl.BlockSpec(memory_space=pltpu.VMEM)
    made = pl.pallas_call(
        lattice_kernel,
        out_shape=(
            pltpu.VMEM((3, 19, ROWS + 2 * PZ, PY), f32),
            pltpu.VMEM((3, ROWS, PY), f32),
            pltpu.VMEM((ROWS, PY), f32),
            pltpu.VMEM((3, ROWS, PY), f32),
            pltpu.VMEM((ROWS, PY), f32),
            pltpu.VMEM((ROWS, PY), jnp.int32),
        ),
        in_specs=[anywhere] * 6,
        out_specs=(vmem,) * 6,
        scratch_shapes=[
            pltpu.VMEM((2, 2, 5, PZ, PY), f32),
            pltpu.VMEM((2, 2, PZ, PY), f32),
            pltpu.VMEM((2, 2, 2, 5, PX // 2, PY), f32),
            pltpu.VMEM((2, 2, PZ, PY), f32),
            pltpu.VMEM((2, 2, PZ, PY), f32),
            pltpu.VMEM((2, len(CORNERS) + 10, PZ, PY), f32),
            pltpu.VMEM((2, len(NEAR), PZ, PY), f32),
            pltpu.VMEM((2, 2, 2, 5, PX // 2, PY), f32),
            pltpu.VMEM((2, PZ, PY), f32),
            dma((6,)),
            dma((2, 5)),
            dma((2, 5)),
        ],
        compiler_params=pltpu.CompilerParams(
            collective_id=0, has_side_effects=True, vmem_limit_bytes=56 * 1024 * 1024
        ),
    )(
        adjoint.reshape(19, ROWS, PY),
        density.reshape(ROWS, PY),
        velocity.reshape(3, ROWS, PY),
        porosity.reshape(ROWS, PY),
        node_type.reshape(ROWS, PY),
        sensitivity_in.reshape(ROWS, PY),
    )
    out, sens = pl.pallas_call(
        last_kernel,
        out_shape=(
            jax.ShapeDtypeStruct((19, ROWS, PY), f32),
            jax.ShapeDtypeStruct((ROWS, PY), f32),
        ),
        in_specs=[vmem] * 6,
        out_specs=(anywhere, anywhere),
        scratch_shapes=[
            pltpu.VMEM((2, 19, PZ, PY), f32),
            pltpu.VMEM((2, PZ, PY), f32),
            dma((6,)),
        ],
        compiler_params=pltpu.CompilerParams(vmem_limit_bytes=8 * 1024 * 1024),
    )(*made)
    return out.reshape(19, PX, PZ, PY), sens.reshape(PX, PZ, PY)


def solution(mesh):
    cells = P("gx", "gz", "gy")
    many = P(None, "gx", "gz", "gy")
    return jax.shard_map(
        shards,
        mesh=mesh,
        in_specs=(many, cells, many, cells, cells, cells),
        out_specs=(many, cells),
        check_vma=False,
    )
```

```python
import functools

import jax
import jax.numpy as jnp
from jax import lax
from jax.experimental import pallas as pl
from jax.experimental.pallas import tpu as pltpu
from jax.sharding import PartitionSpec as P

AXES = ("gx", "gy", "gz")
PX, PZ, PY = 16, 8, 128
ROWS = PX * PZ

VELOCITIES = [
    (0, 0, 0),
    (1, 0, 0),
    (-1, 0, 0),
    (0, 1, 0),
    (0, -1, 0),
    (0, 0, 1),
    (0, 0, -1),
    (1, 1, 0),
    (-1, -1, 0),
    (1, -1, 0),
    (-1, 1, 0),
    (1, 0, 1),
    (-1, 0, -1),
    (1, 0, -1),
    (-1, 0, 1),
    (0, 1, 1),
    (0, -1, -1),
    (0, 1, -1),
    (0, -1, 1),
]
CROSS = [[[i for i, c in enumerate(VELOCITIES) if c[a] == s] for s in (1, -1)] for a in range(3)]
CROSS_X, CROSS_Y, CROSS_Z = CROSS
FACES_X = [(-1, 0, 0), (1, 0, 0)]
FACES_Y = [(0, -1, 0), (0, 1, 0)]
FACES_Z = [(0, 0, -1), (0, 0, 1)]
EDGES_XY = [(a, b, 0) for a in (-1, 1) for b in (-1, 1)]
EDGES_YZ = [(0, a, b) for a in (-1, 1) for b in (-1, 1)]
EDGES_XZ = [(a, 0, b) for a in (-1, 1) for b in (-1, 1)]
FAR = EDGES_XZ + EDGES_XY + FACES_X
NEAR = EDGES_YZ + FACES_Y
ROUTES = FAR + FACES_Z + NEAR
CORNERS = EDGES_XZ + EDGES_XY
GROUP_FAR, GROUP_Z, GROUP_NEAR, GROUP_RELAY = 0, 1, 3, 4
GREETED = FACES_X + FACES_Z + NEAR


def side(sign):
    return (sign + 1) // 2


def collide(p, rho, u, g, node):
    ux, uy, uz = u
    e = [p[i] + p[i + 1] for i in range(1, 19, 2)]
    o = [p[i] - p[i + 1] for i in range(1, 19, 2)]
    sxy, sxz, syz = e[3] + e[4], e[5] + e[6], e[7] + e[8]
    dxy, dxz, dyz = e[3] - e[4], e[5] - e[6], e[7] - e[8]
    sx = 2.0 * e[0] + (sxy + sxz)
    sy = 2.0 * e[1] + (sxy + syz)
    sz = 2.0 * e[2] + (sxz + syz)
    trace = sx + sy + sz
    h36 = 12.0 * p[0] + (trace - (sxy + sxz + syz))
    third = h36 * (1.0 / 3.0)
    mxx, myy, mzz = sx - third, sy - third, sz - third
    hcx = 2.0 * o[0] + ((o[3] + o[4]) + (o[5] + o[6]))
    hcy = 2.0 * o[1] + ((o[3] - o[4]) + (o[7] + o[8]))
    hcz = 2.0 * o[2] + ((o[5] - o[6]) + (o[7] - o[8]))
    nx = mxx * ux + dxy * uy + dxz * uz
    ny = dxy * ux + myy * uy + dyz * uz
    nz = dxz * ux + dyz * uy + mzz * uz
    q = ux * nx + uy * ny + uz * nz
    first = ux * hcx + uy * hcy + uz * hcz
    g4 = 0.4 * g
    b = g4 * g
    a = g * (1.0 / 12.0) + (1.0 / 60.0)
    gain = rho * (first * (1.0 / 12.0) + g4 * q)
    inlet = node == 1
    wall = node == 2
    vx = a * hcx + b * nx + jnp.where(inlet, 1.0, 0.0)
    vy = a * hcy + b * ny
    vz = a * hcz + b * nz
    base = h36 * (1.1 / 36.0) + trace * (1.0 / 120.0) - (0.5 * b) * q
    ex, ey, ez = -0.025 * mxx, -0.025 * myy, -0.025 * mzz
    bx, by = base + ex, base + ey
    bz = base + ez
    bxy, bxz, byz = bx + ey, bx + ez, by + ez
    wxy, wxz, wyz = 0.05 * dxy, 0.05 * dxz, 0.05 * dyz
    even = [bx, by, bz, bxy - wxy, bxy + wxy, bxz - wxz, bxz + wxz, byz - wyz, byz + wyz]
    odd = [vx, vy, vz, vx + vy, vx - vy, vx + vz, vx - vz, vy + vz, vy - vz]
    new = [jnp.where(wall, p[0], base - 0.4 * p[0])]
    for k in range(9):
        up = even[k] - 0.2 * e[k]
        down = odd[k] - 0.1 * o[k]
        new.append(jnp.where(wall, p[2 * k + 2], up + down))
        new.append(jnp.where(wall, p[2 * k + 1], up - down))
    return new, jnp.where(wall, 0.0, gain)


def plane(x):
    if isinstance(x, int):
        return pl.ds(x * PZ, PZ)
    return pl.ds(pl.multiple_of(x * PZ, PZ), PZ)


def advance(old, rows, rho, vel, por, node):
    pulled = []
    for value, (_, _, cz) in zip(old, VELOCITIES):
        if cz:
            value = pltpu.roll(value, PZ - 1 if cz == 1 else 1, axis=0)
        pulled.append(value)
    u = [vel[d, rows, :] for d in range(3)]
    return collide(pulled, rho[rows, :], u, por[rows, :], node[rows, :])


def lattice_kernel(
    adj_hbm,
    rho_hbm,
    vel_hbm,
    por_hbm,
    node_hbm,
    sens_hbm,
    field,
    sens,
    rho,
    vel,
    por,
    node,
    far_in,
    x_out,
    y_out,
    z_out,
    xy_out,
    xz_out,
    near_in,
    z_in,
    relay_in,
    load_sem,
    send_sem,
    recv_sem,
):
    here = [lax.axis_index(a) for a in AXES]
    size = [lax.axis_size(a) for a in AXES]

    def device(route):
        return tuple(lax.rem(h + (d + n), n) if d else h for h, d, n in zip(here, route, size))

    barrier = pltpu.get_barrier_semaphore()
    for route in GREETED:
        pl.semaphore_signal(
            barrier, inc=1, device_id=device(route), device_id_type=pl.DeviceIdType.MESH
        )
    own = pl.ds(PZ, ROWS)
    loads = [
        pltpu.make_async_copy(src, dst, load_sem.at[k])
        for k, (src, dst) in enumerate(
            [
                (adj_hbm, field.at[0, :, own, :]),
                (rho_hbm, rho),
                (vel_hbm, vel),
                (por_hbm, por),
                (node_hbm, node),
                (sens_hbm, sens.at[0]),
            ]
        )
    ]
    for copy in loads:
        copy.start()

    lane = lax.broadcasted_iota(jnp.int32, (PZ, PY), 1)
    row = lax.broadcasted_iota(jnp.int32, (PZ, PY), 0)

    def pack_columns(step, x, tiles):
        made = []
        for s in range(2):
            tile = tiles[s]
            for j, i in enumerate(CROSS_Y[s]):
                at = x + j * PX
                value = field[step, i, plane(x + 1), :]
                turned = pltpu.roll(value, at if s == 0 else at + 1, axis=1)
                tile = jnp.where(lane == at, turned, tile)
            made.append(tile)
        return tuple(made)

    def pull_y(step, i, x, tile, at):
        cy = VELOCITIES[i][1]
        edge = PY - 1 if cy == 1 else 0
        shift = (edge - at) % PY if isinstance(at, int) else (edge or PY) - at
        column = pltpu.roll(tile, shift, axis=1)
        value = pltpu.roll(field[step, i, plane(x + 1), :], PY - 1 if cy == 1 else 1, axis=1)
        field[step, i, plane(x + 1), :] = jnp.where(lane == edge, column, value)

    def x_part(buffer, step, s):
        return buffer.at[step, pl.ds(len(CORNERS) + 5 * s, 5)]

    def copy_of(step, group, src, dst, route):
        return pltpu.make_async_remote_copy(
            src_ref=src,
            dst_ref=dst,
            send_sem=send_sem.at[step, group],
            recv_sem=recv_sem.at[step, group],
            device_id=device(route),
            device_id_type=pl.DeviceIdType.MESH,
        )

    def transfer(step, route, half=0):
        dx, dy, dz = route
        if route in FACES_X:
            src, dst = x_out.at[step, side(dx)], x_part(far_in, step, side(dx))
        elif route in FACES_Z:
            src, dst = z_out.at[step, half, side(dz)], z_in.at[step, half, side(dz)]
        elif route in NEAR:
            src, dst = y_out.at[step, side(dy)], near_in.at[step, NEAR.index(route)]
        elif route in EDGES_XY:
            src, dst = xy_out.at[step, side(dy)], far_in.at[step, CORNERS.index(route)]
        else:
            src, dst = xz_out.at[step, side(dz)], far_in.at[step, CORNERS.index(route)]
        if route in FACES_Z:
            return copy_of(step, GROUP_Z + half, src, dst, route)
        return copy_of(step, GROUP_NEAR if route in NEAR else GROUP_FAR, src, dst, route)

    def whole(step, group):
        if group == GROUP_FAR:
            buffer = far_in.at[step]
        elif group == GROUP_NEAR:
            buffer = near_in.at[step]
        elif group == GROUP_RELAY:
            buffer = relay_in
        else:
            buffer = z_in.at[step, group - GROUP_Z]
        return copy_of(step, group, buffer, buffer, FACES_X[0])

    def pack_xz(step):
        for s in range(2):
            for i in CROSS_Z[s]:
                cx = VELOCITIES[i][0]
                if cx:
                    line = pl.ds(PZ * (1 if cx == 1 else PX) + s * (PZ - 1), 1)
                    xz_out[step, s, pl.ds(side(-cx) * (PZ - 1), 1), :] = field[step, i, line, :]

    def send_corner_rows():
        for s, route in enumerate(FACES_Z):
            copy_of(0, GROUP_RELAY, xz_out.at[0, s], relay_in.at[s], route).start()

    def relay():
        def forward(src, dx, dy, dz):
            dst = far_in.at[0, CORNERS.index((dx, dy, dz))]
            copy_of(0, GROUP_FAR, src, dst, (dx, 0, 0)).start()

        whole(0, GROUP_RELAY).wait_recv()
        for dx in (-1, 1):
            for dz in (-1, 1):
                forward(relay_in.at[side(dz)], dx, 0, dz)
        whole(0, GROUP_NEAR).wait_recv()
        for dx in (-1, 1):
            for dy in (-1, 1):
                forward(near_in.at[0, NEAR.index((0, dy, 0))], dx, dy, 0)

    def pack_x(step, tiles):
        for s in range(2):
            xy_out[step, s] = tiles[s]
            for j, i in enumerate(CROSS_X[s]):
                x_out[step, s, j] = field[step, i, plane(PX if s else 1), :]

    def z_rows(s, half):
        return pl.ds(PZ + s * (PZ - 1) + half * (ROWS // 2), PX // 2, stride=PZ)

    def pack_z(step, half):
        for s in range(2):
            for j, i in enumerate(CROSS_Z[s]):
                z_out[step, half, s, j] = field[step, i, z_rows(s, half), :]

    def send_z(step, half):
        for route in FACES_Z:
            transfer(step, route, half).start()

    def pack_near(step, tiles):
        for s in range(2):
            y_out[step, s] = tiles[s]

    def send(step, routes):
        for route in routes:
            transfer(step, route).start()

    def insert_y(step):
        @pl.when(step == 1)
        def _():
            whole(1, GROUP_NEAR).wait_recv()

        tiles = {}
        for s in range(2):
            for i in CROSS_Y[s]:
                cz = VELOCITIES[i][2]
                tiles[i] = near_in[step, NEAR.index(FACES_Y[s])]
                if cz:
                    corner = near_in[step, NEAR.index((0, 2 * s - 1, -cz))]
                    tiles[i] = jnp.where(row == (0 if cz == 1 else PZ - 1), corner, tiles[i])

        def body(x, carry):
            for s in range(2):
                for j, i in enumerate(CROSS_Y[s]):
                    pull_y(step, i, x, tiles[i], x + j * PX)
            return carry

        lax.fori_loop(0, PX, body, 0, unroll=4)

    def insert_z(step, half):
        whole(step, GROUP_Z + half).wait_recv()
        for s in range(2):
            for j, i in enumerate(CROSS_Z[s]):
                rows = z_rows(s, half)
                value = z_in[step, half, s, j]
                cy = VELOCITIES[i][1]
                if cy:
                    value = pltpu.roll(value, PY - 1 if cy == 1 else 1, axis=1)
                    value = jnp.where(
                        lane == (PY - 1 if cy == 1 else 0), field[step, i, rows, :], value
                    )
                field[step, i, rows, :] = value

    def insert_x(step):
        whole(step, GROUP_FAR).wait_recv()
        for s in range(2):
            for j, i in enumerate(CROSS_X[s]):
                field[step, i, plane(0 if s else PX + 1), :] = far_in[
                    step, len(CORNERS) + 5 * s + j
                ]
        for route in EDGES_XZ:
            dx, _, dz = route
            i = VELOCITIES.index((-dx, 0, -dz))
            at = side(dz) * (PZ - 1)
            field[step, i, pl.ds((0 if dx == 1 else PZ * (PX + 1)) + at, 1), :] = far_in[
                step, CORNERS.index(route), pl.ds(side(dx) * (PZ - 1), 1), :
            ]
        for route in EDGES_XY:
            dx, dy, _ = route
            i = VELOCITIES.index((-dx, -dy, 0))
            at = CROSS_Y[side(dy)].index(i) * PX + (PX - 1 if dx == 1 else 0)
            tile = far_in[step, CORNERS.index(route)]
            pull_y(step, i, -1 if dx == 1 else PX, tile, at)

    def step_plane(step, x):
        old = [field[step, i, plane(x + 1 + c[0]), :] for i, c in enumerate(VELOCITIES)]
        rows = plane(x)
        new, gain = advance(old, rows, rho, vel, por, node)
        for i in range(19):
            field[step + 1, i, plane(x + 1), :] = new[i]
        sens[step + 1, rows, :] = sens[step, rows, :] + gain

    def one_step(step, carry):
        def pair(k, c):
            step_plane(step, 2 * k + 1)
            step_plane(step, 2 * k + 2)
            return c

        insert_y(step)
        insert_z(step, 0)
        insert_z(step, 1)
        lax.fori_loop(0, PX // 2 - 1, pair, 0)

        @pl.when(step == 0)
        def _():
            tiles = (blank,) * 2
            for x in range(1, PX - 1):
                tiles = pack_columns(1, x, tiles)
            insert_x(0)
            for x in (0, PX - 1):
                step_plane(0, x)
            pack_xz(1)
            send(1, EDGES_XZ)
            for x in (0, PX - 1):
                tiles = pack_columns(1, x, tiles)
            pack_x(1, tiles)
            send(1, EDGES_XY + FACES_X)
            pack_z(1, 0)
            pack_z(1, 1)
            send_z(1, 0)
            send_z(1, 1)
            pack_near(1, tiles)
            send(1, NEAR)
            for group in range(5):
                whole(0, group).wait_send()

        return carry

    blank = jnp.zeros((PZ, PY), jnp.float32)
    loads[0].wait()
    tiles = (blank,) * 2
    for x in range(PX):
        tiles = pack_columns(0, x, tiles)
    pack_xz(0)
    pack_x(0, tiles)
    pack_near(0, tiles)
    pack_z(0, 0)
    pack_z(0, 1)
    pl.semaphore_wait(barrier, len(GREETED))
    send_corner_rows()
    send(0, NEAR)
    send_z(0, 0)
    send_z(0, 1)
    send(0, FACES_X)
    for copy in loads[1:]:
        copy.wait()
    relay()
    lax.fori_loop(0, 2, one_step, 0)
    for group in range(4):
        whole(1, group).wait_send()
    whole(1, GROUP_FAR).wait_recv()


def outer_plane(far, i):
    cx, cy, cz = VELOCITIES[i]
    s = side(-cx)
    value = far[1, len(CORNERS) + 5 * s + CROSS_X[s].index(i)]
    if cz:
        line = far[1, CORNERS.index((-cx, 0, -cz)), pl.ds(s * (PZ - 1), 1), :]
        row = lax.broadcasted_iota(jnp.int32, (PZ, PY), 0)
        value = jnp.where(row == side(-cz) * (PZ - 1), line, value)
    if cy:
        edge = PY - 1 if cy == 1 else 0
        at = CROSS_Y[side(-cy)].index(i) * PX + s * (PX - 1)
        lane = lax.broadcasted_iota(jnp.int32, (PZ, PY), 1)
        column = pltpu.roll(far[1, CORNERS.index((-cx, -cy, 0))], (edge - at) % PY, axis=1)
        value = jnp.where(lane == edge, column, pltpu.roll(value, PY - 1 if cy == 1 else 1, axis=1))
    return value


def last_kernel(field, sens, rho, vel, por, node, far, out_hbm, out_sens_hbm, result, gained, sem):
    inner = pl.ds(PZ, ROWS - 2 * PZ)
    copies = [
        pltpu.make_async_copy(
            field.at[2, :, pl.ds(2 * PZ, ROWS - 2 * PZ), :], out_hbm.at[:, inner, :], sem.at[0]
        ),
        pltpu.make_async_copy(sens.at[2, inner, :], out_sens_hbm.at[inner, :], sem.at[1]),
    ]
    for copy in copies:
        copy.start()
    for k, x in enumerate((0, PX - 1)):
        old = []
        for i, (cx, _, _) in enumerate(VELOCITIES):
            if 0 <= x + cx < PX:
                old.append(field[1, i, plane(x + 1 + cx), :])
            else:
                old.append(outer_plane(far, i))
        rows = plane(x)
        new, gain = advance(old, rows, rho, vel, por, node)
        for i in range(19):
            result[k, i] = new[i]
        gained[k] = sens[1, rows, :] + gain
    for k, x in enumerate((0, PX - 1)):
        rows = plane(x)
        copies.append(
            pltpu.make_async_copy(result.at[k], out_hbm.at[:, rows, :], sem.at[2 + 2 * k])
        )
        copies.append(
            pltpu.make_async_copy(gained.at[k], out_sens_hbm.at[rows, :], sem.at[3 + 2 * k])
        )
    for copy in copies[2:]:
        copy.start()
    for copy in copies:
        copy.wait()


def shards(adjoint, density, velocity, porosity, node_type, sensitivity_in):
    f32 = jnp.float32
    dma = pltpu.SemaphoreType.DMA
    anywhere = pl.BlockSpec(memory_space=pl.ANY)
    vmem = pl.BlockSpec(memory_space=pltpu.VMEM)
    made = pl.pallas_call(
        lattice_kernel,
        out_shape=(
            pltpu.VMEM((3, 19, ROWS + 2 * PZ, PY), f32),
            pltpu.VMEM((3, ROWS, PY), f32),
            pltpu.VMEM((ROWS, PY), f32),
            pltpu.VMEM((3, ROWS, PY), f32),
            pltpu.VMEM((ROWS, PY), f32),
            pltpu.VMEM((ROWS, PY), jnp.int32),
            pltpu.VMEM((2, len(CORNERS) + 10, PZ, PY), f32),
        ),
        in_specs=[anywhere] * 6,
        out_specs=(vmem,) * 7,
        scratch_shapes=[
            pltpu.VMEM((2, 2, 5, PZ, PY), f32),
            pltpu.VMEM((2, 2, PZ, PY), f32),
            pltpu.VMEM((2, 2, 2, 5, PX // 2, PY), f32),
            pltpu.VMEM((2, 2, PZ, PY), f32),
            pltpu.VMEM((2, 2, PZ, PY), f32),
            pltpu.VMEM((2, len(NEAR), PZ, PY), f32),
            pltpu.VMEM((2, 2, 2, 5, PX // 2, PY), f32),
            pltpu.VMEM((2, PZ, PY), f32),
            dma((6,)),
            dma((2, 5)),
            dma((2, 5)),
        ],
        compiler_params=pltpu.CompilerParams(
            collective_id=0, has_side_effects=True, vmem_limit_bytes=56 * 1024 * 1024
        ),
    )(
        adjoint.reshape(19, ROWS, PY),
        density.reshape(ROWS, PY),
        velocity.reshape(3, ROWS, PY),
        porosity.reshape(ROWS, PY),
        node_type.reshape(ROWS, PY),
        sensitivity_in.reshape(ROWS, PY),
    )
    out, sens = pl.pallas_call(
        last_kernel,
        out_shape=(
            jax.ShapeDtypeStruct((19, ROWS, PY), f32),
            jax.ShapeDtypeStruct((ROWS, PY), f32),
        ),
        in_specs=[vmem] * 7,
        out_specs=(anywhere, anywhere),
        scratch_shapes=[
            pltpu.VMEM((2, 19, PZ, PY), f32),
            pltpu.VMEM((2, PZ, PY), f32),
            dma((6,)),
        ],
        compiler_params=pltpu.CompilerParams(vmem_limit_bytes=8 * 1024 * 1024),
    )(*made)
    return out.reshape(19, PX, PZ, PY), sens.reshape(PX, PZ, PY)


def solution(mesh):
    cells = P("gx", "gz", "gy")
    many = P(None, "gx", "gz", "gy")
    return jax.shard_map(
        shards,
        mesh=mesh,
        in_specs=(many, cells, many, cells, cells, cells),
        out_specs=(many, cells),
        check_vma=False,
    )
```

```python
import functools

import jax
import jax.numpy as jnp
from jax import lax
from jax.experimental import pallas as pl
from jax.experimental.pallas import tpu as pltpu
from jax.sharding import PartitionSpec as P

AXES = ("gx", "gy", "gz")
PX, PZ, PY = 16, 8, 128
ROWS = PX * PZ

VELOCITIES = [
    (0, 0, 0),
    (1, 0, 0),
    (-1, 0, 0),
    (0, 1, 0),
    (0, -1, 0),
    (0, 0, 1),
    (0, 0, -1),
    (1, 1, 0),
    (-1, -1, 0),
    (1, -1, 0),
    (-1, 1, 0),
    (1, 0, 1),
    (-1, 0, -1),
    (1, 0, -1),
    (-1, 0, 1),
    (0, 1, 1),
    (0, -1, -1),
    (0, 1, -1),
    (0, -1, 1),
]
CROSS = [[[i for i, c in enumerate(VELOCITIES) if c[a] == s] for s in (1, -1)] for a in range(3)]
CROSS_X, CROSS_Y, CROSS_Z = CROSS
FACES_X = [(-1, 0, 0), (1, 0, 0)]
FACES_Y = [(0, -1, 0), (0, 1, 0)]
FACES_Z = [(0, 0, -1), (0, 0, 1)]
EDGES_XY = [(a, b, 0) for a in (-1, 1) for b in (-1, 1)]
EDGES_YZ = [(0, a, b) for a in (-1, 1) for b in (-1, 1)]
EDGES_XZ = [(a, 0, b) for a in (-1, 1) for b in (-1, 1)]
FAR = EDGES_XZ + EDGES_XY + FACES_X
NEAR = EDGES_YZ + FACES_Y
ROUTES = FAR + FACES_Z + NEAR
CORNERS = EDGES_XZ + EDGES_XY
GROUP_FAR, GROUP_Z, GROUP_NEAR, GROUP_RELAY = 0, 1, 2, 3
GREETED = FACES_X + FACES_Z + NEAR


def side(sign):
    return (sign + 1) // 2


def collide(p, rho, u, g, node):
    ux, uy, uz = u
    e = [p[i] + p[i + 1] for i in range(1, 19, 2)]
    o = [p[i] - p[i + 1] for i in range(1, 19, 2)]
    sxy, sxz, syz = e[3] + e[4], e[5] + e[6], e[7] + e[8]
    dxy, dxz, dyz = e[3] - e[4], e[5] - e[6], e[7] - e[8]
    sx = 2.0 * e[0] + (sxy + sxz)
    sy = 2.0 * e[1] + (sxy + syz)
    sz = 2.0 * e[2] + (sxz + syz)
    trace = sx + sy + sz
    h36 = 12.0 * p[0] + (trace - (sxy + sxz + syz))
    third = h36 * (1.0 / 3.0)
    mxx, myy, mzz = sx - third, sy - third, sz - third
    hcx = 2.0 * o[0] + ((o[3] + o[4]) + (o[5] + o[6]))
    hcy = 2.0 * o[1] + ((o[3] - o[4]) + (o[7] + o[8]))
    hcz = 2.0 * o[2] + ((o[5] - o[6]) + (o[7] - o[8]))
    nx = mxx * ux + dxy * uy + dxz * uz
    ny = dxy * ux + myy * uy + dyz * uz
    nz = dxz * ux + dyz * uy + mzz * uz
    q = ux * nx + uy * ny + uz * nz
    first = ux * hcx + uy * hcy + uz * hcz
    g4 = 0.4 * g
    b = g4 * g
    a = g * (1.0 / 12.0) + (1.0 / 60.0)
    gain = rho * (first * (1.0 / 12.0) + g4 * q)
    inlet = node == 1
    wall = node == 2
    vx = a * hcx + b * nx + jnp.where(inlet, 1.0, 0.0)
    vy = a * hcy + b * ny
    vz = a * hcz + b * nz
    base = h36 * (1.1 / 36.0) + trace * (1.0 / 120.0) - (0.5 * b) * q
    ex, ey, ez = -0.025 * mxx, -0.025 * myy, -0.025 * mzz
    bx, by = base + ex, base + ey
    bz = base + ez
    bxy, bxz, byz = bx + ey, bx + ez, by + ez
    wxy, wxz, wyz = 0.05 * dxy, 0.05 * dxz, 0.05 * dyz
    even = [bx, by, bz, bxy - wxy, bxy + wxy, bxz - wxz, bxz + wxz, byz - wyz, byz + wyz]
    odd = [vx, vy, vz, vx + vy, vx - vy, vx + vz, vx - vz, vy + vz, vy - vz]
    new = [jnp.where(wall, p[0], base - 0.4 * p[0])]
    for k in range(9):
        up = even[k] - 0.2 * e[k]
        down = odd[k] - 0.1 * o[k]
        new.append(jnp.where(wall, p[2 * k + 2], up + down))
        new.append(jnp.where(wall, p[2 * k + 1], up - down))
    return new, jnp.where(wall, 0.0, gain)


def plane(x):
    if isinstance(x, int):
        return pl.ds(x * PZ, PZ)
    return pl.ds(pl.multiple_of(x * PZ, PZ), PZ)


def advance(old, rows, rho, vel, por, node):
    pulled = []
    for value, (_, _, cz) in zip(old, VELOCITIES):
        if cz:
            value = pltpu.roll(value, PZ - 1 if cz == 1 else 1, axis=0)
        pulled.append(value)
    u = [vel[d, rows, :] for d in range(3)]
    return collide(pulled, rho[rows, :], u, por[rows, :], node[rows, :])


def lattice_kernel(
    adj_hbm,
    rho_hbm,
    vel_hbm,
    por_hbm,
    node_hbm,
    sens_hbm,
    field,
    sens,
    rho,
    vel,
    por,
    node,
    far_in,
    x_out,
    y_out,
    z_out,
    xy_out,
    xz_out,
    near_in,
    z_in,
    relay_in,
    load_sem,
    send_sem,
    recv_sem,
):
    here = [lax.axis_index(a) for a in AXES]
    size = [lax.axis_size(a) for a in AXES]

    def device(route):
        return tuple(lax.rem(h + (d + n), n) if d else h for h, d, n in zip(here, route, size))

    barrier = pltpu.get_barrier_semaphore()
    for route in GREETED:
        pl.semaphore_signal(
            barrier, inc=1, device_id=device(route), device_id_type=pl.DeviceIdType.MESH
        )
    own = pl.ds(PZ, ROWS)
    loads = [
        pltpu.make_async_copy(src, dst, load_sem.at[k])
        for k, (src, dst) in enumerate(
            [
                (adj_hbm, field.at[0, :, own, :]),
                (rho_hbm, rho),
                (vel_hbm, vel),
                (por_hbm, por),
                (node_hbm, node),
                (sens_hbm, sens.at[0]),
            ]
        )
    ]
    for copy in loads:
        copy.start()

    lane = lax.broadcasted_iota(jnp.int32, (PZ, PY), 1)
    row = lax.broadcasted_iota(jnp.int32, (PZ, PY), 0)

    def pack_columns(step, x, tiles):
        made = []
        for s in range(2):
            tile = tiles[s]
            for j, i in enumerate(CROSS_Y[s]):
                at = x + j * PX
                value = field[step, i, plane(x + 1), :]
                turned = pltpu.roll(value, at if s == 0 else at + 1, axis=1)
                tile = jnp.where(lane == at, turned, tile)
            made.append(tile)
        return tuple(made)

    def pull_y(step, i, x, tile, at):
        cy = VELOCITIES[i][1]
        edge = PY - 1 if cy == 1 else 0
        shift = (edge - at) % PY if isinstance(at, int) else (edge or PY) - at
        column = pltpu.roll(tile, shift, axis=1)
        value = pltpu.roll(field[step, i, plane(x + 1), :], PY - 1 if cy == 1 else 1, axis=1)
        field[step, i, plane(x + 1), :] = jnp.where(lane == edge, column, value)

    def x_part(buffer, step, s):
        return buffer.at[step, pl.ds(len(CORNERS) + 5 * s, 5)]

    def copy_of(step, group, src, dst, route):
        return pltpu.make_async_remote_copy(
            src_ref=src,
            dst_ref=dst,
            send_sem=send_sem.at[step, group],
            recv_sem=recv_sem.at[step, group],
            device_id=device(route),
            device_id_type=pl.DeviceIdType.MESH,
        )

    def transfer(step, route):
        dx, dy, dz = route
        if route in FACES_X:
            src, dst = x_out.at[step, side(dx)], x_part(far_in, step, side(dx))
        elif route in FACES_Z:
            src, dst = z_out.at[step, side(dz)], z_in.at[step, side(dz)]
        elif route in NEAR:
            src, dst = y_out.at[step, side(dy)], near_in.at[step, NEAR.index(route)]
        elif route in EDGES_XY:
            src, dst = xy_out.at[step, side(dy)], far_in.at[step, CORNERS.index(route)]
        else:
            src, dst = xz_out.at[step, side(dz)], far_in.at[step, CORNERS.index(route)]
        if route in FACES_Z:
            return copy_of(step, GROUP_Z, src, dst, route)
        return copy_of(step, GROUP_NEAR if route in NEAR else GROUP_FAR, src, dst, route)

    def whole(step, group):
        if group == GROUP_FAR:
            buffer = far_in.at[step]
        elif group == GROUP_NEAR:
            buffer = near_in.at[step]
        elif group == GROUP_RELAY:
            buffer = relay_in
        else:
            buffer = z_in.at[step]
        return copy_of(step, group, buffer, buffer, FACES_X[0])

    def pack_xz(step):
        for s in range(2):
            for i in CROSS_Z[s]:
                cx = VELOCITIES[i][0]
                if cx:
                    line = pl.ds(PZ * (1 if cx == 1 else PX) + s * (PZ - 1), 1)
                    xz_out[step, s, pl.ds(side(-cx) * (PZ - 1), 1), :] = field[step, i, line, :]

    def send_corner_rows():
        for s, route in enumerate(FACES_Z):
            copy_of(0, GROUP_RELAY, xz_out.at[0, s], relay_in.at[s], route).start()

    def relay():
        def forward(src, dx, dy, dz):
            dst = far_in.at[0, CORNERS.index((dx, dy, dz))]
            copy_of(0, GROUP_FAR, src, dst, (dx, 0, 0)).start()

        whole(0, GROUP_RELAY).wait_recv()
        for dx in (-1, 1):
            for dz in (-1, 1):
                forward(relay_in.at[side(dz)], dx, 0, dz)
        whole(0, GROUP_NEAR).wait_recv()
        for dx in (-1, 1):
            for dy in (-1, 1):
                forward(near_in.at[0, NEAR.index((0, dy, 0))], dx, dy, 0)

    def pack_x(step, tiles):
        for s in range(2):
            xy_out[step, s] = tiles[s]
            for j, i in enumerate(CROSS_X[s]):
                x_out[step, s, j] = field[step, i, plane(PX if s else 1), :]

    def z_rows(s):
        return pl.ds(PZ + s * (PZ - 1), PX, stride=PZ)

    def pack_z(step):
        for s in range(2):
            for j, i in enumerate(CROSS_Z[s]):
                z_out[step, s, j] = field[step, i, z_rows(s), :]

    def send_z(step):
        for route in FACES_Z:
            transfer(step, route).start()

    def pack_near(step, tiles):
        for s in range(2):
            y_out[step, s] = tiles[s]

    def send(step, routes):
        for route in routes:
            transfer(step, route).start()

    def insert_y(step):
        @pl.when(step == 1)
        def _():
            whole(1, GROUP_NEAR).wait_recv()

        tiles = {}
        for s in range(2):
            for i in CROSS_Y[s]:
                cz = VELOCITIES[i][2]
                tiles[i] = near_in[step, NEAR.index(FACES_Y[s])]
                if cz:
                    corner = near_in[step, NEAR.index((0, 2 * s - 1, -cz))]
                    tiles[i] = jnp.where(row == (0 if cz == 1 else PZ - 1), corner, tiles[i])

        def body(x, carry):
            for s in range(2):
                for j, i in enumerate(CROSS_Y[s]):
                    pull_y(step, i, x, tiles[i], x + j * PX)
            return carry

        lax.fori_loop(0, PX, body, 0, unroll=4)

    def insert_z(step):
        wide = lax.broadcasted_iota(jnp.int32, (PX, PY), 1)
        whole(step, GROUP_Z).wait_recv()
        for s in range(2):
            for j, i in enumerate(CROSS_Z[s]):
                rows = z_rows(s)
                value = z_in[step, s, j]
                cy = VELOCITIES[i][1]
                if cy:
                    value = pltpu.roll(value, PY - 1 if cy == 1 else 1, axis=1)
                    value = jnp.where(
                        wide == (PY - 1 if cy == 1 else 0), field[step, i, rows, :], value
                    )
                field[step, i, rows, :] = value

    def insert_x(step):
        whole(step, GROUP_FAR).wait_recv()
        for s in range(2):
            for j, i in enumerate(CROSS_X[s]):
                field[step, i, plane(0 if s else PX + 1), :] = far_in[
                    step, len(CORNERS) + 5 * s + j
                ]
        for route in EDGES_XZ:
            dx, _, dz = route
            i = VELOCITIES.index((-dx, 0, -dz))
            at = side(dz) * (PZ - 1)
            field[step, i, pl.ds((0 if dx == 1 else PZ * (PX + 1)) + at, 1), :] = far_in[
                step, CORNERS.index(route), pl.ds(side(dx) * (PZ - 1), 1), :
            ]
        for route in EDGES_XY:
            dx, dy, _ = route
            i = VELOCITIES.index((-dx, -dy, 0))
            at = CROSS_Y[side(dy)].index(i) * PX + (PX - 1 if dx == 1 else 0)
            tile = far_in[step, CORNERS.index(route)]
            pull_y(step, i, -1 if dx == 1 else PX, tile, at)

    def step_plane(step, x):
        old = [field[step, i, plane(x + 1 + c[0]), :] for i, c in enumerate(VELOCITIES)]
        rows = plane(x)
        new, gain = advance(old, rows, rho, vel, por, node)
        for i in range(19):
            field[step + 1, i, plane(x + 1), :] = new[i]
        sens[step + 1, rows, :] = sens[step, rows, :] + gain

    def one_step(step, carry):
        def pair(k, c):
            step_plane(step, 2 * k + 1)
            step_plane(step, 2 * k + 2)
            return c

        insert_y(step)
        insert_z(step)
        lax.fori_loop(0, PX // 2 - 1, pair, 0)

        @pl.when(step == 0)
        def _():
            tiles = (blank,) * 2
            for x in range(1, PX - 1):
                tiles = pack_columns(1, x, tiles)
            insert_x(0)
            for x in (0, PX - 1):
                step_plane(0, x)
            pack_xz(1)
            send(1, EDGES_XZ)
            for x in (0, PX - 1):
                tiles = pack_columns(1, x, tiles)
            pack_x(1, tiles)
            send(1, EDGES_XY + FACES_X)
            pack_z(1)
            send_z(1)
            pack_near(1, tiles)
            send(1, NEAR)
            for group in range(4):
                whole(0, group).wait_send()

        return carry

    blank = jnp.zeros((PZ, PY), jnp.float32)
    loads[0].wait()
    tiles = (blank,) * 2
    for x in range(PX):
        tiles = pack_columns(0, x, tiles)
    pack_xz(0)
    pack_x(0, tiles)
    pack_near(0, tiles)
    pack_z(0)
    pl.semaphore_wait(barrier, len(GREETED))
    send_corner_rows()
    send(0, NEAR)
    send_z(0)
    send(0, FACES_X)
    for copy in loads[1:]:
        copy.wait()
    relay()
    lax.fori_loop(0, 2, one_step, 0)
    for group in range(3):
        whole(1, group).wait_send()
    whole(1, GROUP_FAR).wait_recv()


def outer_plane(far, i):
    cx, cy, cz = VELOCITIES[i]
    s = side(-cx)
    value = far[1, len(CORNERS) + 5 * s + CROSS_X[s].index(i)]
    if cz:
        line = far[1, CORNERS.index((-cx, 0, -cz)), pl.ds(s * (PZ - 1), 1), :]
        row = lax.broadcasted_iota(jnp.int32, (PZ, PY), 0)
        value = jnp.where(row == side(-cz) * (PZ - 1), line, value)
    if cy:
        edge = PY - 1 if cy == 1 else 0
        at = CROSS_Y[side(-cy)].index(i) * PX + s * (PX - 1)
        lane = lax.broadcasted_iota(jnp.int32, (PZ, PY), 1)
        column = pltpu.roll(far[1, CORNERS.index((-cx, -cy, 0))], (edge - at) % PY, axis=1)
        value = jnp.where(lane == edge, column, pltpu.roll(value, PY - 1 if cy == 1 else 1, axis=1))
    return value


def last_kernel(field, sens, rho, vel, por, node, far, out_hbm, out_sens_hbm, result, gained, sem):
    inner = pl.ds(PZ, ROWS - 2 * PZ)
    copies = [
        pltpu.make_async_copy(
            field.at[2, :, pl.ds(2 * PZ, ROWS - 2 * PZ), :], out_hbm.at[:, inner, :], sem.at[0]
        ),
        pltpu.make_async_copy(sens.at[2, inner, :], out_sens_hbm.at[inner, :], sem.at[1]),
    ]
    for copy in copies:
        copy.start()
    for k, x in enumerate((0, PX - 1)):
        old = []
        for i, (cx, _, _) in enumerate(VELOCITIES):
            if 0 <= x + cx < PX:
                old.append(field[1, i, plane(x + 1 + cx), :])
            else:
                old.append(outer_plane(far, i))
        rows = plane(x)
        new, gain = advance(old, rows, rho, vel, por, node)
        for i in range(19):
            result[k, i] = new[i]
        gained[k] = sens[1, rows, :] + gain
    for k, x in enumerate((0, PX - 1)):
        rows = plane(x)
        copies.append(
            pltpu.make_async_copy(result.at[k], out_hbm.at[:, rows, :], sem.at[2 + 2 * k])
        )
        copies.append(
            pltpu.make_async_copy(gained.at[k], out_sens_hbm.at[rows, :], sem.at[3 + 2 * k])
        )
    for copy in copies[2:]:
        copy.start()
    for copy in copies:
        copy.wait()


def shards(adjoint, density, velocity, porosity, node_type, sensitivity_in):
    f32 = jnp.float32
    dma = pltpu.SemaphoreType.DMA
    anywhere = pl.BlockSpec(memory_space=pl.ANY)
    vmem = pl.BlockSpec(memory_space=pltpu.VMEM)
    made = pl.pallas_call(
        lattice_kernel,
        out_shape=(
            pltpu.VMEM((3, 19, ROWS + 2 * PZ, PY), f32),
            pltpu.VMEM((3, ROWS, PY), f32),
            pltpu.VMEM((ROWS, PY), f32),
            pltpu.VMEM((3, ROWS, PY), f32),
            pltpu.VMEM((ROWS, PY), f32),
            pltpu.VMEM((ROWS, PY), jnp.int32),
            pltpu.VMEM((2, len(CORNERS) + 10, PZ, PY), f32),
        ),
        in_specs=[anywhere] * 6,
        out_specs=(vmem,) * 7,
        scratch_shapes=[
            pltpu.VMEM((2, 2, 5, PZ, PY), f32),
            pltpu.VMEM((2, 2, PZ, PY), f32),
            pltpu.VMEM((2, 2, 5, PX, PY), f32),
            pltpu.VMEM((2, 2, PZ, PY), f32),
            pltpu.VMEM((2, 2, PZ, PY), f32),
            pltpu.VMEM((2, len(NEAR), PZ, PY), f32),
            pltpu.VMEM((2, 2, 5, PX, PY), f32),
            pltpu.VMEM((2, PZ, PY), f32),
            dma((6,)),
            dma((2, 4)),
            dma((2, 4)),
        ],
        compiler_params=pltpu.CompilerParams(
            collective_id=0, has_side_effects=True, vmem_limit_bytes=56 * 1024 * 1024
        ),
    )(
        adjoint.reshape(19, ROWS, PY),
        density.reshape(ROWS, PY),
        velocity.reshape(3, ROWS, PY),
        porosity.reshape(ROWS, PY),
        node_type.reshape(ROWS, PY),
        sensitivity_in.reshape(ROWS, PY),
    )
    out, sens = pl.pallas_call(
        last_kernel,
        out_shape=(
            jax.ShapeDtypeStruct((19, ROWS, PY), f32),
            jax.ShapeDtypeStruct((ROWS, PY), f32),
        ),
        in_specs=[vmem] * 7,
        out_specs=(anywhere, anywhere),
        scratch_shapes=[
            pltpu.VMEM((2, 19, PZ, PY), f32),
            pltpu.VMEM((2, PZ, PY), f32),
            dma((6,)),
        ],
        compiler_params=pltpu.CompilerParams(vmem_limit_bytes=8 * 1024 * 1024),
    )(*made)
    return out.reshape(19, PX, PZ, PY), sens.reshape(PX, PZ, PY)


def solution(mesh):
    cells = P("gx", "gz", "gy")
    many = P(None, "gx", "gz", "gy")
    return jax.shard_map(
        shards,
        mesh=mesh,
        in_specs=(many, cells, many, cells, cells, cells),
        out_specs=(many, cells),
        check_vma=False,
    )
```
